32 devices in a mesh: lag: 16 (over z, y, x), par: 2 (over core).
Axes of the slice: x: 2, y: 2, z: 4, core: 2. Of those that a mesh axis runs over, the one named last changes fastest.
Arguments:
- prior_rows: bfloat16 [16, 512, 4096], P('lag', None, 'par'), may hold values from -0.125 to 0.125
- raw_rows: bfloat16 [16, 512, 4096], P('lag', None, 'par'), may hold values from -6 to 6
Outputs:
- diag_zero: float32 [16, 512, 512], P('lag', 'par')
- diag_one: float32 [16, 512, 512], P('lag', 'par')
The draws below stay inside these ranges and needn't reach their ends.
All inputs are finite; a program needn't handle non-finite values.
Results may differ from the reference program's by a relative error of at most 0.0003.
Values may be sent and summed in bfloat16 or wider, within the bound.
A program may use at most 64 MiB of HBM per device.

```python
import jax
import jax.numpy as jnp
from jax import lax

SENSORS = 512
LAGS = 16
PANEL = 4096


def with_spikes(result, key, source, target, shards_of, factor):
    owner, partner = [(jnp.arange(result.shape[position]) // (result.shape[position] // shards_of)).reshape([-1 if axis == position else 1 for axis in range(result.ndim)]) for position in (source, target)]
    chosen = jax.random.permutation(key, shards_of)[partner]
    strong = (owner == chosen) | (owner == (partner + shards_of // 2) % shards_of)
    return jnp.where(strong, factor * result, result)


def block_scale(key, extent, shards, smallest, top_value):
    def one(position, parts):
        heights = jax.random.uniform(jax.random.fold_in(jax.random.fold_in(key, 6), position), (parts,), jnp.float32, smallest / len(shards), top_value / len(shards))
        return jnp.repeat(jnp.exp(heights), extent[position] // parts).reshape((-1,) + (1,) * (len(extent) - position - 1))

    loudness = one(*shards[0])
    for cut in shards[1:]:
        loudness = loudness * one(*cut)
    return loudness


def normal_values(rng, extent, scale, limit, pieces=(), kind=jnp.bfloat16):
    array = scale * jax.random.normal(rng, extent, jnp.float32)
    if pieces:
        array = array * block_scale(rng, extent, pieces, -0.22, 0.18)
    return jnp.clip(array, -limit, limit).astype(kind)


def bell_draw_with(own_key, dims, spread, bound, pieces, heavy, kind=jnp.bfloat16):
    result = spread * jax.random.normal(own_key, dims, jnp.float32)
    if pieces:
        result = result * block_scale(own_key, dims, pieces, -0.22, 0.18)
    return jnp.clip(with_spikes(result, jax.random.fold_in(own_key, 3), *heavy), -bound, bound).astype(kind)


def setup_inputs(seed: int = 0) -> dict:
    arg_keys = jax.random.split(jax.random.key(seed), 3)
    return {
        "prior_rows": bell_draw_with(arg_keys[0], (LAGS, SENSORS, PANEL), PANEL ** -0.5, 0.125, ((0, 16), (2, 2)), (2, 1, 2, 2.0)),
        "raw_rows": normal_values(arg_keys[1], (LAGS, SENSORS, PANEL), 1.0, 6.0, ((0, 16), (2, 2))),
    }


def lag_tiles(blocks):
    prior_block, raw_block, next_block = blocks
    tile_zero = jnp.dot(prior_block, raw_block.T, preferred_element_type=jnp.float32)
    tile_one = jnp.dot(prior_block, next_block.T, preferred_element_type=jnp.float32)
    return tile_zero, tile_one


def reference(prior_rows, raw_rows):
    following = jnp.concatenate([raw_rows[1:], jnp.zeros_like(raw_rows[:1])], axis=0)
    tile_zero, tile_one = lax.map(lag_tiles, (prior_rows, raw_rows, following))
    return jnp.cumsum(tile_zero, axis=0), jnp.cumsum(tile_one, axis=0)
```

```python
import functools

import jax
import jax.numpy as jnp
from jax import lax
from jax.experimental import pallas as pl
from jax.experimental.pallas import tpu as pltpu
from jax.sharding import PartitionSpec as P

MESH = pl.DeviceIdType.MESH
SENT = jnp.float32


def group_size(lags, rows):
    best = 1
    for size in range(1, lags + 1):
        if lags % size == 0 and size * size <= lags and rows % (16 * size) == 0:
            best = size
    return best


def kernel(
    lags, pars, members, zero_items, one_items,
    prior_hbm, raw_hbm, zero_out, one_out,
    prior, raw, coming,
    zero_part, zero_met, zero_tile, zero_mates, zero_groups, zero_ahead, zero_first, zero_back,
    one_part, one_met, one_tile, one_mates, one_groups, one_ahead, one_first, one_back,
    load_sem, shift_send, shift_recv,
    zero_sems, one_sems,
):
    lag = lax.axis_index("lag")
    par = lax.axis_index("par")
    groups = lags // members
    group = lag // members
    member = lax.rem(lag, members)
    base = group * members

    loads = [
        pltpu.make_async_copy(prior_hbm.at[0], prior, load_sem.at[0]),
        pltpu.make_async_copy(raw_hbm.at[0], raw, load_sem.at[1]),
    ]
    for load in loads:
        load.start()

    barrier = pltpu.get_barrier_semaphore()

    def greet(other_lag, other_par):
        pl.semaphore_signal(barrier, inc=1, device_id=(other_lag, other_par), device_id_type=MESH)

    for step in range(1, pars):
        greet(lag, lax.rem(par + step, pars))
    for step in range(1, members):
        greet(base + lax.rem(member + step, members), par)
    for step in range(1, groups):
        greet(lax.rem(group + step, groups) * members + member, par)

    @pl.when(lag > 0)
    def _():
        greet(lag - 1, par)

    @pl.when(lag < lags - 1)
    def _():
        greet(lag + 1, par)

    fixed = (pars - 1) + (members - 1) + (groups - 1)
    pl.semaphore_wait(barrier, fixed + jnp.minimum(lag, 1) + jnp.minimum(lags - 1 - lag, 1))

    span = raw.shape[0] // one_items

    def shift(item):
        rows = pl.ds(item * span, span)
        return pltpu.make_async_remote_copy(
            src_ref=raw_hbm.at[0, rows],
            dst_ref=coming.at[rows],
            send_sem=shift_send.at[item],
            recv_sem=shift_recv.at[item],
            device_id=(lag - 1, par),
            device_id_type=MESH,
        )

    @pl.when(lag > 0)
    def _():
        for item in range(one_items):
            shift(item).start()

    def lag_sums(item, rows_ref, out_ref, part, met, tile, mates, totals, ahead, first, back, sems):
        (part_send, part_recv, mate_send, mate_recv, group_send, group_recv, back_send, back_recv) = sems
        pending = []
        width = part.shape[-1]
        share = part.shape[2]
        quarter = tile.shape[2]
        columns = pl.ds(item * width, width)
        product = lax.dot_general(
            prior[...], rows_ref[columns, :], (((1,), (1,)), ((), ())),
            preferred_element_type=jnp.float32,
        )
        for owner in range(pars):
            part[item, owner] = product[owner * share:(owner + 1) * share]

        def to_peer(step):
            peer = lax.rem(par + step, pars)
            return pltpu.make_async_remote_copy(
                src_ref=part.at[item, peer],
                dst_ref=met.at[item, step - 1],
                send_sem=part_send.at[item, step - 1],
                recv_sem=part_recv.at[item, step - 1],
                device_id=(lag, peer),
                device_id_type=MESH,
            )

        for step in range(1, pars):
            copy = to_peer(step)
            copy.start()
            pending.append(copy)
        total = part[item, par]
        for step in range(1, pars):
            to_peer(step).wait_recv()
            total = total + met[item, step - 1]
        for owner in range(members):
            tile[item, owner] = total[owner * quarter:(owner + 1) * quarter]

        def to_mate(step):
            mate = lax.rem(member + step, members)
            return pltpu.make_async_remote_copy(
                src_ref=tile.at[item, mate],
                dst_ref=mates.at[item, member],
                send_sem=mate_send.at[item, mate],
                recv_sem=mate_recv.at[item, member],
                device_id=(base + mate, par),
                device_id_type=MESH,
            )

        def from_mate(step):
            mate = lax.rem(member + step, members)
            return pltpu.make_async_remote_copy(
                src_ref=tile.at[item, mate],
                dst_ref=mates.at[item, mate],
                send_sem=mate_send.at[item, mate],
                recv_sem=mate_recv.at[item, mate],
                device_id=(base + mate, par),
                device_id_type=MESH,
            )

        for step in range(1, members):
            copy = to_mate(step)
            copy.start()
            pending.append(copy)
        mates[item, member] = tile[item, member]
        for step in range(1, members):
            from_mate(step).wait_recv()

        total = mates[item, 0]
        for mate in range(1, members):
            total = total + mates[item, mate]
        totals[item] = total

        def to_group(step):
            return pltpu.make_async_remote_copy(
                src_ref=totals.at[item],
                dst_ref=ahead.at[item, step - 1],
                send_sem=group_send.at[item, step - 1],
                recv_sem=group_recv.at[item, step - 1],
                device_id=((group + step) * members + member, par),
                device_id_type=MESH,
            )

        for step in range(1, groups):
            @pl.when(group + step < groups)
            def _():
                to_group(step).start()

        first[item, 0] = jnp.zeros_like(total)
        for step in range(1, groups):
            @pl.when(group >= step)
            def _():
                to_group(step).wait_recv()
                first[item, 0] += ahead[item, step - 1]
        for mate in range(1, members):
            first[item, mate] = first[item, mate - 1] + mates[item, mate - 1]

        def to_member(step):
            mate = lax.rem(member + step, members)
            return pltpu.make_async_remote_copy(
                src_ref=first.at[item, mate],
                dst_ref=back.at[item, member],
                send_sem=back_send.at[item, mate],
                recv_sem=back_recv.at[item, member],
                device_id=(base + mate, par),
                device_id_type=MESH,
            )

        def from_member(step):
            mate = lax.rem(member + step, members)
            return pltpu.make_async_remote_copy(
                src_ref=first.at[item, mate],
                dst_ref=back.at[item, mate],
                send_sem=back_send.at[item, mate],
                recv_sem=back_recv.at[item, mate],
                device_id=(base + mate, par),
                device_id_type=MESH,
            )

        for step in range(1, members):
            copy = to_member(step)
            copy.start()
            pending.append(copy)
        back[item, member] = first[item, member]
        for step in range(1, members):
            from_member(step).wait_recv()
        for owner in range(members):
            out_ref[0, owner * quarter:(owner + 1) * quarter, item * width:(item + 1) * width] = (
                back[item, owner] + tile[item, owner]
            )

        def finish():
            for copy in pending:
                copy.wait_send()
            for step in range(1, groups):
                @pl.when(group + step < groups)
                def _():
                    to_group(step).wait_send()

        return finish

    for load in loads:
        load.wait()
    ends = []
    for item in range(zero_items):
        ends.append(lag_sums(
            item, raw, zero_out, zero_part, zero_met, zero_tile, zero_mates,
            zero_groups, zero_ahead, zero_first, zero_back, zero_sems,
        ))
    for item in range(one_items):
        @pl.when(lag < lags - 1)
        def _():
            shift(item).wait_recv()

        @pl.when(lag == lags - 1)
        def _():
            rows = pl.ds(item * span, span)
            coming[rows, :] = jnp.zeros((span, coming.shape[1]), coming.dtype)

        ends.append(lag_sums(
            item, coming, one_out, one_part, one_met, one_tile, one_mates,
            one_groups, one_ahead, one_first, one_back, one_sems,
        ))
    for end in ends:
        end()

    @pl.when(lag > 0)
    def _():
        for item in range(one_items):
            shift(item).wait_send()


def scratch_of(items, lags, pars, members, sensors):
    width, share = sensors // items, sensors // pars
    quarter, groups = share // members, lags // members
    f32 = jnp.float32
    buffers = [
        pltpu.VMEM((items, pars, share, width), f32),
        pltpu.VMEM((items, max(pars - 1, 1), share, width), f32),
        pltpu.VMEM((items, members, quarter, width), f32),
        pltpu.VMEM((items, members, quarter, width), f32),
        pltpu.VMEM((items, quarter, width), f32),
        pltpu.VMEM((items, max(groups - 1, 1), quarter, width), f32),
        pltpu.VMEM((items, members, quarter, width), f32),
        pltpu.VMEM((items, members, quarter, width), f32),
    ]
    counts = (pars, pars, members, members, groups, groups, members, members)
    return buffers, tuple(pltpu.SemaphoreType.DMA((items, count)) for count in counts)


def solution(mesh):
    lags, pars = mesh.shape["lag"], mesh.shape["par"]

    def body(prior_rows, raw_rows):
        sensors, panel = prior_rows.shape[1:]
        share = sensors // pars
        members = group_size(lags, share)
        zero_items, one_items = 1, 4
        zero_buffers, zero_sems = scratch_of(zero_items, lags, pars, members, sensors)
        one_buffers, one_sems = scratch_of(one_items, lags, pars, members, sensors)
        out = jax.ShapeDtypeStruct((1, share, sensors), jnp.float32)
        return pl.pallas_call(
            functools.partial(kernel, lags, pars, members, zero_items, one_items),
            out_shape=(out, out),
            in_specs=[pl.BlockSpec(memory_space=pl.ANY)] * 2,
            out_specs=[pl.BlockSpec(memory_space=pltpu.VMEM)] * 2,
            scratch_shapes=[
                pltpu.VMEM((sensors, panel), jnp.bfloat16),
                pltpu.VMEM((sensors, panel), jnp.bfloat16),
                pltpu.VMEM((sensors, panel), jnp.bfloat16),
                *zero_buffers,
                *one_buffers,
                pltpu.SemaphoreType.DMA((2,)),
                pltpu.SemaphoreType.DMA((one_items,)),
                pltpu.SemaphoreType.DMA((one_items,)),
                zero_sems,
                one_sems,
            ],
            compiler_params=pltpu.CompilerParams(
                collective_id=0, has_side_effects=True, vmem_limit_bytes=48 * 2**20
            ),
            cost_estimate=pl.CostEstimate(
                flops=4 * sensors * sensors * panel,
                bytes_accessed=4 * sensors * panel + 8 * share * sensors,
                transcendentals=0,
            ),
        )(prior_rows, raw_rows)

    in_specs = (P("lag", None, "par"), P("lag", None, "par"))
    out_specs = (P("lag", "par", None), P("lag", "par", None))
    return jax.shard_map(body, mesh=mesh, in_specs=in_specs, out_specs=out_specs, check_vma=False)
```

```python
import functools

import jax
import jax.numpy as jnp
from jax import lax
from jax.experimental import pallas as pl
from jax.experimental.pallas import tpu as pltpu
from jax.sharding import PartitionSpec as P

MESH = pl.DeviceIdType.MESH
SENT = jnp.float32


def group_size(lags, rows):
    best = 1
    for size in range(1, lags + 1):
        if lags % size == 0 and size * size <= lags and rows % (16 * size) == 0:
            best = size
    return best


def kernel(
    lags, pars, members, one_items,
    prior_hbm, raw_hbm, zero_out, one_out,
    prior, raw, coming,
    zero_part, zero_met, zero_tile, zero_mates, zero_groups, zero_ahead, zero_first, zero_back,
    one_part, one_met, one_tile, one_mates, one_groups, one_ahead, one_first, one_back,
    load_sem, shift_send, shift_recv,
    zero_sems, one_sems,
):
    lag = lax.axis_index("lag")
    par = lax.axis_index("par")
    groups = lags // members
    group = lag // members
    member = lax.rem(lag, members)
    base = group * members

    loads = [
        pltpu.make_async_copy(prior_hbm.at[0], prior, load_sem.at[0]),
        pltpu.make_async_copy(raw_hbm.at[0], raw, load_sem.at[1]),
    ]
    for load in loads:
        load.start()

    barrier = pltpu.get_barrier_semaphore()

    def greet(other_lag, other_par):
        pl.semaphore_signal(barrier, inc=1, device_id=(other_lag, other_par), device_id_type=MESH)

    for step in range(1, pars):
        greet(lag, lax.rem(par + step, pars))
    for step in range(1, members):
        greet(base + lax.rem(member + step, members), par)
    for step in range(1, groups):
        greet(lax.rem(group + step, groups) * members + member, par)

    @pl.when(lag > 0)
    def _():
        greet(lag - 1, par)

    @pl.when(lag < lags - 1)
    def _():
        greet(lag + 1, par)

    fixed = (pars - 1) + (members - 1) + (groups - 1)
    pl.semaphore_wait(barrier, fixed + jnp.minimum(lag, 1) + jnp.minimum(lags - 1 - lag, 1))

    span = raw.shape[0] // one_items

    def shift(item):
        rows = pl.ds(item * span, span)
        return pltpu.make_async_remote_copy(
            src_ref=raw_hbm.at[0, rows],
            dst_ref=coming.at[rows],
            send_sem=shift_send.at[item],
            recv_sem=shift_recv.at[item],
            device_id=(lag - 1, par),
            device_id_type=MESH,
        )

    def stages_of(item, rows_ref, out_ref, part, met, tile, mates, totals, ahead, first, back, sems):
        (part_send, part_recv, mate_send, mate_recv, group_send, group_recv, back_send, back_recv) = sems
        width = part.shape[-1]
        share = part.shape[2]
        quarter = tile.shape[2]

        def to_peer(step):
            peer = lax.rem(par + step, pars)
            return pltpu.make_async_remote_copy(
                src_ref=part.at[item, peer],
                dst_ref=met.at[item, step - 1],
                send_sem=part_send.at[item, step - 1],
                recv_sem=part_recv.at[item, step - 1],
                device_id=(lag, peer),
                device_id_type=MESH,
            )

        def among(source, target, send_sem, recv_sem, step, incoming):
            mate = lax.rem(member + step, members)
            place = mate if incoming else member
            return pltpu.make_async_remote_copy(
                src_ref=source.at[item, mate],
                dst_ref=target.at[item, place],
                send_sem=send_sem.at[item, mate],
                recv_sem=recv_sem.at[item, place],
                device_id=(base + mate, par),
                device_id_type=MESH,
            )

        gather = functools.partial(among, tile, mates, mate_send, mate_recv)
        give = functools.partial(among, first, back, back_send, back_recv)

        def to_group(step):
            return pltpu.make_async_remote_copy(
                src_ref=totals.at[item],
                dst_ref=ahead.at[item, step - 1],
                send_sem=group_send.at[item, step - 1],
                recv_sem=group_recv.at[item, step - 1],
                device_id=((group + step) * members + member, par),
                device_id_type=MESH,
            )

        def multiply():
            product = lax.dot_general(
                prior[...], rows_ref[pl.ds(item * width, width), :], (((1,), (1,)), ((), ())),
                preferred_element_type=jnp.float32,
            )
            for owner in range(pars):
                part[item, owner] = product[owner * share:(owner + 1) * share]
            for step in range(1, pars):
                to_peer(step).start()

        def sum_peers():
            total = part[item, par]
            for step in range(1, pars):
                to_peer(step).wait_recv()
                total = total + met[item, step - 1]
            for owner in range(members):
                tile[item, owner] = total[owner * quarter:(owner + 1) * quarter]
            for step in range(1, members):
                gather(step, False).start()
            mates[item, member] = tile[item, member]

        def sum_group():
            for step in range(1, members):
                gather(step, True).wait_recv()
            total = mates[item, 0]
            for mate in range(1, members):
                total = total + mates[item, mate]
            totals[item] = total
            for step in range(1, groups):
                @pl.when(group + step < groups)
                def _():
                    to_group(step).start()

        def sum_before():
            first[item, 0] = jnp.zeros_like(totals[item])
            for step in range(1, groups):
                @pl.when(group >= step)
                def _():
                    to_group(step).wait_recv()
                    first[item, 0] += ahead[item, step - 1]
            for mate in range(1, members):
                first[item, mate] = first[item, mate - 1] + mates[item, mate - 1]
            for step in range(1, members):
                give(step, False).start()
            back[item, member] = first[item, member]

        def store():
            for step in range(1, members):
                give(step, True).wait_recv()
            for owner in range(members):
                out_ref[0, owner * quarter:(owner + 1) * quarter, item * width:(item + 1) * width] = (
                    back[item, owner] + tile[item, owner]
                )

        def finish():
            for step in range(1, pars):
                to_peer(step).wait_send()
            for step in range(1, members):
                gather(step, False).wait_send()
                give(step, False).wait_send()
            for step in range(1, groups):
                @pl.when(group + step < groups)
                def _():
                    to_group(step).wait_send()

        return multiply, sum_peers, sum_group, sum_before, store, finish

    def arrive(item):
        @pl.when(lag < lags - 1)
        def _():
            shift(item).wait_recv()

        @pl.when(lag == lags - 1)
        def _():
            rows = pl.ds(item * span, span)
            coming[rows, :] = jnp.zeros((span, coming.shape[1]), coming.dtype)

    def depart(item):
        @pl.when(lag > 0)
        def _():
            shift(item).start()

    zero = stages_of(
        0, raw, zero_out, zero_part, zero_met, zero_tile, zero_mates,
        zero_groups, zero_ahead, zero_first, zero_back, zero_sems,
    )
    ones = [
        stages_of(
            item, coming, one_out, one_part, one_met, one_tile, one_mates,
            one_groups, one_ahead, one_first, one_back, one_sems,
        )
        for item in range(one_items)
    ]
    lines = [zero] + ones

    depart(0)
    depart(1)
    for load in loads:
        load.wait()
    for turn, line in enumerate(lines):
        if turn >= 1:
            arrive(turn - 1)
        line[0]()
        line[1]()
        if turn >= 1:
            lines[turn - 1][3]()
        if turn + 2 < one_items:
            depart(turn + 2)
        if turn >= 2:
            lines[turn - 2][4]()
        line[2]()
    lines[-1][3]()
    lines[-2][4]()
    lines[-1][4]()
    for line in lines:
        line[5]()

    @pl.when(lag > 0)
    def _():
        for item in range(one_items):
            shift(item).wait_send()


def scratch_of(items, lags, pars, members, sensors):
    width, share = sensors // items, sensors // pars
    quarter, groups = share // members, lags // members
    f32 = jnp.float32
    buffers = [
        pltpu.VMEM((items, pars, share, width), f32),
        pltpu.VMEM((items, max(pars - 1, 1), share, width), f32),
        pltpu.VMEM((items, members, quarter, width), f32),
        pltpu.VMEM((items, members, quarter, width), f32),
        pltpu.VMEM((items, quarter, width), f32),
        pltpu.VMEM((items, max(groups - 1, 1), quarter, width), f32),
        pltpu.VMEM((items, members, quarter, width), f32),
        pltpu.VMEM((items, members, quarter, width), f32),
    ]
    counts = (pars, pars, members, members, groups, groups, members, members)
    return buffers, tuple(pltpu.SemaphoreType.DMA((items, count)) for count in counts)


def solution(mesh):
    lags, pars = mesh.shape["lag"], mesh.shape["par"]

    def body(prior_rows, raw_rows):
        sensors, panel = prior_rows.shape[1:]
        share = sensors // pars
        members = group_size(lags, share)
        one_items = 4
        zero_buffers, zero_sems = scratch_of(1, lags, pars, members, sensors)
        one_buffers, one_sems = scratch_of(one_items, lags, pars, members, sensors)
        out = jax.ShapeDtypeStruct((1, share, sensors), jnp.float32)
        return pl.pallas_call(
            functools.partial(kernel, lags, pars, members, one_items),
            out_shape=(out, out),
            in_specs=[pl.BlockSpec(memory_space=pl.ANY)] * 2,
            out_specs=[pl.BlockSpec(memory_space=pltpu.VMEM)] * 2,
            scratch_shapes=[
                pltpu.VMEM((sensors, panel), jnp.bfloat16),
                pltpu.VMEM((sensors, panel), jnp.bfloat16),
                pltpu.VMEM((sensors, panel), jnp.bfloat16),
                *zero_buffers,
                *one_buffers,
                pltpu.SemaphoreType.DMA((2,)),
                pltpu.SemaphoreType.DMA((one_items,)),
                pltpu.SemaphoreType.DMA((one_items,)),
                zero_sems,
                one_sems,
            ],
            compiler_params=pltpu.CompilerParams(
                collective_id=0, has_side_effects=True, vmem_limit_bytes=60 * 2**20
            ),
            cost_estimate=pl.CostEstimate(
                flops=4 * sensors * sensors * panel,
                bytes_accessed=4 * sensors * panel + 8 * share * sensors,
                transcendentals=0,
            ),
        )(prior_rows, raw_rows)

    in_specs = (P("lag", None, "par"), P("lag", None, "par"))
    out_specs = (P("lag", "par", None), P("lag", "par", None))
    return jax.shard_map(body, mesh=mesh, in_specs=in_specs, out_specs=out_specs, check_vma=False)
```

```python
import functools

import jax
import jax.numpy as jnp
from jax import lax
from jax.experimental import pallas as pl
from jax.experimental.pallas import tpu as pltpu
from jax.sharding import PartitionSpec as P

MESH = pl.DeviceIdType.MESH
SENT = jnp.float32


def group_size(lags, rows):
    best = 1
    for size in range(1, lags + 1):
        if lags % size == 0 and size * size <= lags and rows % (16 * size) == 0:
            best = size
    return best


def kernel(
    lags, pars, members, zero_items, one_items,
    prior_hbm, raw_hbm, zero_out, one_out,
    prior, raw, coming,
    zero_part, zero_met, zero_tile, zero_mates, zero_groups, zero_ahead, zero_first, zero_back,
    one_part, one_met, one_tile, one_mates, one_groups, one_ahead, one_first, one_back,
    load_sem, shift_send, shift_recv,
    zero_sems, one_sems,
):
    lag = lax.axis_index("lag")
    par = lax.axis_index("par")
    groups = lags // members
    group = lag // members
    member = lax.rem(lag, members)
    base = group * members

    loads = [
        pltpu.make_async_copy(prior_hbm.at[0], prior, load_sem.at[0]),
        pltpu.make_async_copy(raw_hbm.at[0], raw, load_sem.at[1]),
    ]
    for load in loads:
        load.start()

    barrier = pltpu.get_barrier_semaphore()

    def greet(other_lag, other_par):
        pl.semaphore_signal(barrier, inc=1, device_id=(other_lag, other_par), device_id_type=MESH)

    for step in range(1, pars):
        greet(lag, lax.rem(par + step, pars))
    for step in range(1, members):
        greet(base + lax.rem(member + step, members), par)
    met_by = (pars - 1) + (members - 1)
    for reach in (1, members):
        @pl.when(lag >= reach)
        def _():
            greet(lag - reach, par)

        @pl.when(lag < lags - reach)
        def _():
            greet(lag + reach, par)

        met_by = met_by + (lag >= reach).astype(jnp.int32) + (lag < lags - reach).astype(jnp.int32)
    pl.semaphore_wait(barrier, met_by)

    span = raw.shape[0] // one_items

    def shift(item):
        rows = pl.ds(item * span, span)
        return pltpu.make_async_remote_copy(
            src_ref=raw_hbm.at[0, rows],
            dst_ref=coming.at[rows],
            send_sem=shift_send.at[item],
            recv_sem=shift_recv.at[item],
            device_id=(lag - 1, par),
            device_id_type=MESH,
        )

    def stages_of(item, rows_ref, out_ref, part, met, tile, mates, totals, ahead, first, back, sems):
        (part_send, part_recv, mate_send, mate_recv, group_send, group_recv, back_send, back_recv) = sems
        width = part.shape[-1]
        share = part.shape[2]
        quarter = tile.shape[2]

        def to_peer(step):
            peer = lax.rem(par + step, pars)
            return pltpu.make_async_remote_copy(
                src_ref=part.at[item, peer],
                dst_ref=met.at[item, step - 1],
                send_sem=part_send.at[item, step - 1],
                recv_sem=part_recv.at[item, step - 1],
                device_id=(lag, peer),
                device_id_type=MESH,
            )

        def among(source, target, send_sem, recv_sem, step, incoming):
            mate = lax.rem(member + step, members)
            place = mate if incoming else member
            return pltpu.make_async_remote_copy(
                src_ref=source.at[item, mate],
                dst_ref=target.at[item, place],
                send_sem=send_sem.at[item, mate],
                recv_sem=recv_sem.at[item, place],
                device_id=(base + mate, par),
                device_id_type=MESH,
            )

        gather = functools.partial(among, tile, mates, mate_send, mate_recv)
        give = functools.partial(among, first, back, back_send, back_recv)

        def to_group():
            return pltpu.make_async_remote_copy(
                src_ref=totals.at[item],
                dst_ref=ahead.at[item],
                send_sem=group_send.at[item],
                recv_sem=group_recv.at[item],
                device_id=(lag + members, par),
                device_id_type=MESH,
            )

        def multiply():
            product = lax.dot_general(
                prior[...], rows_ref[pl.ds(item * width, width), :], (((1,), (1,)), ((), ())),
                preferred_element_type=jnp.float32,
            )
            for owner in range(pars):
                part[item, owner] = product[owner * share:(owner + 1) * share]
            for step in range(1, pars):
                to_peer(step).start()

        def sum_peers():
            total = part[item, par]
            for step in range(1, pars):
                to_peer(step).wait_recv()
                total = total + met[item, step - 1]
            for owner in range(members):
                tile[item, owner] = total[owner * quarter:(owner + 1) * quarter]
            for step in range(1, members):
                gather(step, False).start()
            mates[item, member] = tile[item, member]

        def sum_before():
            for step in range(1, members):
                gather(step, True).wait_recv()

            @pl.when(group == 0)
            def _():
                first[item, 0] = jnp.zeros_like(totals[item])

            @pl.when(group > 0)
            def _():
                to_group().wait_recv()
                first[item, 0] = ahead[item]

            before = first[item, 0]
            for mate in range(1, members):
                before = before + mates[item, mate - 1]
                first[item, mate] = before
            totals[item] = before + mates[item, members - 1]

            @pl.when(group < groups - 1)
            def _():
                to_group().start()

            for step in range(1, members):
                give(step, False).start()
            back[item, member] = first[item, member]

        def store():
            for step in range(1, members):
                give(step, True).wait_recv()
            for owner in range(members):
                out_ref[0, owner * quarter:(owner + 1) * quarter, item * width:(item + 1) * width] = (
                    back[item, owner] + tile[item, owner]
                )

        def finish():
            for step in range(1, pars):
                to_peer(step).wait_send()
            for step in range(1, members):
                gather(step, False).wait_send()
                give(step, False).wait_send()

            @pl.when(group < groups - 1)
            def _():
                to_group().wait_send()

        return multiply, sum_peers, sum_before, store, finish

    def arrive(item):
        @pl.when(lag < lags - 1)
        def _():
            shift(item).wait_recv()

        @pl.when(lag == lags - 1)
        def _():
            rows = pl.ds(item * span, span)
            coming[rows, :] = jnp.zeros((span, coming.shape[1]), coming.dtype)

    def depart(item):
        @pl.when(lag > 0)
        def _():
            shift(item).start()

    zeros = [
        stages_of(
            item, raw, zero_out, zero_part, zero_met, zero_tile, zero_mates,
            zero_groups, zero_ahead, zero_first, zero_back, zero_sems,
        )
        for item in range(zero_items)
    ]
    ones = [
        stages_of(
            item, coming, one_out, one_part, one_met, one_tile, one_mates,
            one_groups, one_ahead, one_first, one_back, one_sems,
        )
        for item in range(one_items)
    ]
    lines = zeros + ones

    for item in range(one_items):
        depart(item)
    for load in loads:
        load.wait()
    for multiply, _, _, _, _ in zeros:
        multiply()
    for _, sum_peers, _, _, _ in zeros:
        sum_peers()
    for item, (multiply, sum_peers, _, _, _) in enumerate(ones):
        arrive(item)
        multiply()
        sum_peers()
    for _, _, sum_before, _, _ in lines:
        sum_before()
    for _, _, _, store, _ in lines:
        store()
    for _, _, _, _, finish in lines:
        finish()

    @pl.when(lag > 0)
    def _():
        for item in range(one_items):
            shift(item).wait_send()


def scratch_of(items, lags, pars, members, sensors):
    width, share = sensors // items, sensors // pars
    quarter = share // members
    f32 = jnp.float32
    buffers = [
        pltpu.VMEM((items, pars, share, width), f32),
        pltpu.VMEM((items, max(pars - 1, 1), share, width), f32),
        pltpu.VMEM((items, members, quarter, width), f32),
        pltpu.VMEM((items, members, quarter, width), f32),
        pltpu.VMEM((items, quarter, width), f32),
        pltpu.VMEM((items, quarter, width), f32),
        pltpu.VMEM((items, members, quarter, width), f32),
        pltpu.VMEM((items, members, quarter, width), f32),
    ]
    shapes = [(items, pars)] * 2 + [(items, members)] * 2 + [(items,)] * 2 + [(items, members)] * 2
    return buffers, tuple(pltpu.SemaphoreType.DMA(shape) for shape in shapes)


def solution(mesh):
    lags, pars = mesh.shape["lag"], mesh.shape["par"]

    def body(prior_rows, raw_rows):
        sensors, panel = prior_rows.shape[1:]
        share = sensors // pars
        members = group_size(lags, share)
        zero_items, one_items = 4, 4
        zero_buffers, zero_sems = scratch_of(zero_items, lags, pars, members, sensors)
        one_buffers, one_sems = scratch_of(one_items, lags, pars, members, sensors)
        out = jax.ShapeDtypeStruct((1, share, sensors), jnp.float32)
        return pl.pallas_call(
            functools.partial(kernel, lags, pars, members, zero_items, one_items),
            out_shape=(out, out),
            in_specs=[pl.BlockSpec(memory_space=pl.ANY)] * 2,
            out_specs=[pl.BlockSpec(memory_space=pltpu.VMEM)] * 2,
            scratch_shapes=[
                pltpu.VMEM((sensors, panel), jnp.bfloat16),
                pltpu.VMEM((sensors, panel), jnp.bfloat16),
                pltpu.VMEM((sensors, panel), jnp.bfloat16),
                *zero_buffers,
                *one_buffers,
                pltpu.SemaphoreType.DMA((2,)),
                pltpu.SemaphoreType.DMA((one_items,)),
                pltpu.SemaphoreType.DMA((one_items,)),
                zero_sems,
                one_sems,
            ],
            compiler_params=pltpu.CompilerParams(
                collective_id=0, has_side_effects=True, vmem_limit_bytes=60 * 2**20
            ),
            cost_estimate=pl.CostEstimate(
                flops=4 * sensors * sensors * panel,
                bytes_accessed=4 * sensors * panel + 8 * share * sensors,
                transcendentals=0,
            ),
        )(prior_rows, raw_rows)

    in_specs = (P("lag", None, "par"), P("lag", None, "par"))
    out_specs = (P("lag", "par", None), P("lag", "par", None))
    return jax.shard_map(body, mesh=mesh, in_specs=in_specs, out_specs=out_specs, check_vma=False)
```

```python
import functools

import jax
import jax.numpy as jnp
from jax import lax
from jax.experimental import pallas as pl
from jax.experimental.pallas import tpu as pltpu
from jax.sharding import PartitionSpec as P

MESH = pl.DeviceIdType.MESH
SENT = jnp.float32


def group_size(lags, rows):
    best = 1
    for size in range(1, lags + 1):
        if lags % size == 0 and size * size <= lags and rows % (16 * size) == 0:
            best = size
    return best


def kernel(
    lags, pars, members, zero_items, one_items,
    prior_hbm, raw_hbm, zero_out, one_out,
    prior, raw, coming,
    zero_part, zero_met, zero_tile, zero_mates, zero_groups, zero_ahead, zero_first, zero_back,
    one_part, one_met, one_tile, one_mates, one_groups, one_ahead, one_first, one_back,
    load_sem, shift_send, shift_recv,
    zero_sems, one_sems,
):
    lag = lax.axis_index("lag")
    par = lax.axis_index("par")
    groups = lags // members
    group = lag // members
    member = lax.rem(lag, members)
    base = group * members

    loads = [
        pltpu.make_async_copy(prior_hbm.at[0], prior, load_sem.at[0]),
        pltpu.make_async_copy(raw_hbm.at[0], raw, load_sem.at[1]),
    ]
    for load in loads:
        load.start()

    barrier = pltpu.get_barrier_semaphore()

    def greet(other_lag, other_par):
        pl.semaphore_signal(barrier, inc=1, device_id=(other_lag, other_par), device_id_type=MESH)

    for step in range(1, pars):
        greet(lag, lax.rem(par + step, pars))
    for step in range(1, members):
        greet(base + lax.rem(member + step, members), par)
    met_by = (pars - 1) + (members - 1)
    for reach in (1, members):
        @pl.when(lag >= reach)
        def _():
            greet(lag - reach, par)

        @pl.when(lag < lags - reach)
        def _():
            greet(lag + reach, par)

        met_by = met_by + (lag >= reach).astype(jnp.int32) + (lag < lags - reach).astype(jnp.int32)
    pl.semaphore_wait(barrier, met_by)

    span = raw.shape[0] // one_items

    def shift(item):
        rows = pl.ds(item * span, span)
        return pltpu.make_async_remote_copy(
            src_ref=raw_hbm.at[0, rows],
            dst_ref=coming.at[rows],
            send_sem=shift_send.at[item],
            recv_sem=shift_recv.at[item],
            device_id=(lag - 1, par),
            device_id_type=MESH,
        )

    def stages_of(item, rows_ref, out_ref, part, met, tile, mates, totals, ahead, first, back, sems):
        (part_send, part_recv, mate_send, mate_recv, group_send, group_recv, back_send, back_recv) = sems
        width = part.shape[-1]
        share = part.shape[2]
        quarter = tile.shape[2]

        def to_peer(step):
            peer = lax.rem(par + step, pars)
            return pltpu.make_async_remote_copy(
                src_ref=part.at[item, peer],
                dst_ref=met.at[item, step - 1],
                send_sem=part_send.at[item, step - 1],
                recv_sem=part_recv.at[item, step - 1],
                device_id=(lag, peer),
                device_id_type=MESH,
            )

        def among(source, target, send_sem, recv_sem, step, incoming):
            mate = lax.rem(member + step, members)
            place = mate if incoming else member
            return pltpu.make_async_remote_copy(
                src_ref=source.at[item, mate],
                dst_ref=target.at[item, place],
                send_sem=send_sem.at[item, mate],
                recv_sem=recv_sem.at[item, place],
                device_id=(base + mate, par),
                device_id_type=MESH,
            )

        gather = functools.partial(among, tile, mates, mate_send, mate_recv)
        give = functools.partial(among, first, back, back_send, back_recv)

        def to_group():
            return pltpu.make_async_remote_copy(
                src_ref=totals.at[item],
                dst_ref=ahead.at[item],
                send_sem=group_send.at[item],
                recv_sem=group_recv.at[item],
                device_id=(lag + members, par),
                device_id_type=MESH,
            )

        def multiply():
            product = lax.dot_general(
                prior[...], rows_ref[pl.ds(item * width, width), :], (((1,), (1,)), ((), ())),
                preferred_element_type=jnp.float32,
            )
            for owner in range(pars):
                part[item, owner] = product[owner * share:(owner + 1) * share]
            for step in range(1, pars):
                to_peer(step).start()

        def sum_peers():
            total = part[item, par]
            for step in range(1, pars):
                to_peer(step).wait_recv()
                total = total + met[item, step - 1]
            for owner in range(members):
                tile[item, owner] = total[owner * quarter:(owner + 1) * quarter]
            for step in range(1, members):
                gather(step, False).start()
            mates[item, member] = tile[item, member]

        def sum_before():
            for step in range(1, members):
                gather(step, True).wait_recv()

            @pl.when(group == 0)
            def _():
                first[item, 0] = jnp.zeros_like(totals[item])

            @pl.when(group > 0)
            def _():
                to_group().wait_recv()
                first[item, 0] = ahead[item]

            before = first[item, 0]
            for mate in range(1, members):
                before = before + mates[item, mate - 1]
                first[item, mate] = before
            totals[item] = before + mates[item, members - 1]

            @pl.when(group < groups - 1)
            def _():
                to_group().start()

            for step in range(1, members):
                give(step, False).start()
            back[item, member] = first[item, member]

        def store():
            for step in range(1, members):
                give(step, True).wait_recv()
            for owner in range(members):
                out_ref[0, owner * quarter:(owner + 1) * quarter, item * width:(item + 1) * width] = (
                    back[item, owner] + tile[item, owner]
                )

        def finish():
            for step in range(1, pars):
                to_peer(step).wait_send()
            for step in range(1, members):
                gather(step, False).wait_send()
                give(step, False).wait_send()

            @pl.when(group < groups - 1)
            def _():
                to_group().wait_send()

        return multiply, sum_peers, sum_before, store, finish

    def arrive(item):
        @pl.when(lag < lags - 1)
        def _():
            shift(item).wait_recv()

        @pl.when(lag == lags - 1)
        def _():
            rows = pl.ds(item * span, span)
            coming[rows, :] = jnp.zeros((span, coming.shape[1]), coming.dtype)

    def depart(item):
        @pl.when(lag > 0)
        def _():
            shift(item).start()

    zeros = [
        stages_of(
            item, raw, zero_out, zero_part, zero_met, zero_tile, zero_mates,
            zero_groups, zero_ahead, zero_first, zero_back, zero_sems,
        )
        for item in range(zero_items)
    ]
    ones = [
        stages_of(
            item, coming, one_out, one_part, one_met, one_tile, one_mates,
            one_groups, one_ahead, one_first, one_back, one_sems,
        )
        for item in range(one_items)
    ]
    lines = zeros + ones

    for item in range(one_items):
        depart(item)
    for load in loads:
        load.wait()
    for multiply, _, _, _, _ in zeros:
        multiply()
    for _, sum_peers, _, _, _ in zeros:
        sum_peers()
    for item, (multiply, sum_peers, _, _, _) in enumerate(ones):
        arrive(item)
        multiply()
        sum_peers()
        if item == one_items - 2:
            for _, _, sum_before, _, _ in zeros:
                sum_before()
    for _, _, sum_before, _, _ in ones:
        sum_before()
    for _, _, _, store, _ in lines:
        store()
    for _, _, _, _, finish in lines:
        finish()

    @pl.when(lag > 0)
    def _():
        for item in range(one_items):
            shift(item).wait_send()


def scratch_of(items, lags, pars, members, sensors):
    width, share = sensors // items, sensors // pars
    quarter = share // members
    f32 = jnp.float32
    buffers = [
        pltpu.VMEM((items, pars, share, width), f32),
        pltpu.VMEM((items, max(pars - 1, 1), share, width), f32),
        pltpu.VMEM((items, members, quarter, width), f32),
        pltpu.VMEM((items, members, quarter, width), f32),
        pltpu.VMEM((items, quarter, width), f32),
        pltpu.VMEM((items, quarter, width), f32),
        pltpu.VMEM((items, members, quarter, width), f32),
        pltpu.VMEM((items, members, quarter, width), f32),
    ]
    shapes = [(items, pars)] * 2 + [(items, members)] * 2 + [(items,)] * 2 + [(items, members)] * 2
    return buffers, tuple(pltpu.SemaphoreType.DMA(shape) for shape in shapes)


def solution(mesh):
    lags, pars = mesh.shape["lag"], mesh.shape["par"]

    def body(prior_rows, raw_rows):
        sensors, panel = prior_rows.shape[1:]
        share = sensors // pars
        members = group_size(lags, share)
        zero_items, one_items = 4, 4
        zero_buffers, zero_sems = scratch_of(zero_items, lags, pars, members, sensors)
        one_buffers, one_sems = scratch_of(one_items, lags, pars, members, sensors)
        out = jax.ShapeDtypeStruct((1, share, sensors), jnp.float32)
        return pl.pallas_call(
            functools.partial(kernel, lags, pars, members, zero_items, one_items),
            out_shape=(out, out),
            in_specs=[pl.BlockSpec(memory_space=pltpu.HBM)] * 2,
            out_specs=[pl.BlockSpec(memory_space=pltpu.VMEM)] * 2,
            scratch_shapes=[
                pltpu.VMEM((sensors, panel), jnp.bfloat16),
                pltpu.VMEM((sensors, panel), jnp.bfloat16),
                pltpu.VMEM((sensors, panel), jnp.bfloat16),
                *zero_buffers,
                *one_buffers,
                pltpu.SemaphoreType.DMA((2,)),
                pltpu.SemaphoreType.DMA((one_items,)),
                pltpu.SemaphoreType.DMA((one_items,)),
                zero_sems,
                one_sems,
            ],
            compiler_params=pltpu.CompilerParams(
                collective_id=0, has_side_effects=True, vmem_limit_bytes=32 * 2**20
            ),
            cost_estimate=pl.CostEstimate(
                flops=4 * sensors * sensors * panel,
                bytes_accessed=4 * sensors * panel + 8 * share * sensors,
                transcendentals=0,
            ),
        )(prior_rows, raw_rows)

    in_specs = (P("lag", None, "par"), P("lag", None, "par"))
    out_specs = (P("lag", "par", None), P("lag", "par", None))
    return jax.shard_map(body, mesh=mesh, in_specs=in_specs, out_specs=out_specs, check_vma=False)
```

```python
import functools

import jax
import jax.numpy as jnp
from jax import lax
from jax.experimental import pallas as pl
from jax.experimental.pallas import tpu as pltpu
from jax.sharding import PartitionSpec as P

MESH = pl.DeviceIdType.MESH
TOP = 240.0


def coded(values):
    scale = jnp.max(jnp.abs(values), axis=0, keepdims=True)
    power = values * (TOP / jnp.maximum(scale, 1e-36))
    negative = power < 0
    for _ in range(4):
        power = power * power
    return jnp.where(negative, -power, power).astype(jnp.bfloat16), scale * (1.0 / TOP)


def decoded(code, scale):
    code = code.astype(jnp.float32)
    root = jnp.maximum(jnp.abs(code), 2e-38)
    for _ in range(4):
        root = lax.rsqrt(root)
    root = root * scale
    return jnp.where(code == 0, 0.0, jnp.where(code < 0, -root, root))


def group_size(lags, rows):
    best = 1
    for size in range(1, lags + 1):
        if lags % size == 0 and size * size <= lags and rows % (16 * size) == 0:
            best = size
    return best


def kernel(
    lags, pars, members, zero_items, one_items,
    prior_hbm, raw_hbm, zero_out, one_out,
    prior, raw, coming,
    zero_buffers, one_buffers,
    load_sem, shift_send, shift_recv,
    zero_sems, one_sems,
):
    lag = lax.axis_index("lag")
    par = lax.axis_index("par")
    groups = lags // members
    group = lag // members
    member = lax.rem(lag, members)
    base = group * members

    loads = [
        pltpu.make_async_copy(prior_hbm.at[0], prior, load_sem.at[0]),
        pltpu.make_async_copy(raw_hbm.at[0], raw, load_sem.at[1]),
    ]
    for load in loads:
        load.start()

    barrier = pltpu.get_barrier_semaphore()

    def greet(other_lag, other_par):
        pl.semaphore_signal(barrier, inc=1, device_id=(other_lag, other_par), device_id_type=MESH)

    for step in range(1, pars):
        greet(lag, lax.rem(par + step, pars))
    for step in range(1, members):
        greet(base + lax.rem(member + step, members), par)
    met_by = (pars - 1) + (members - 1)
    for reach in (1, members):
        @pl.when(lag >= reach)
        def _():
            greet(lag - reach, par)

        @pl.when(lag < lags - reach)
        def _():
            greet(lag + reach, par)

        met_by = met_by + (lag >= reach).astype(jnp.int32) + (lag < lags - reach).astype(jnp.int32)
    pl.semaphore_wait(barrier, met_by)

    span = raw.shape[0] // one_items

    def shift(item):
        rows = pl.ds(item * span, span)
        return pltpu.make_async_remote_copy(
            src_ref=raw_hbm.at[0, rows],
            dst_ref=coming.at[rows],
            send_sem=shift_send.at[item],
            recv_sem=shift_recv.at[item],
            device_id=(lag - 1, par),
            device_id_type=MESH,
        )

    def stages_of(item, rows_ref, out_ref, buffers, sems):
        (part, met, tile, mates, totals, ahead, first, back) = buffers[:8]
        (tile_code, tile_scale, mates_code, mates_scale) = buffers[8:12]
        (first_code, first_scale, back_code, back_scale) = buffers[12:]
        (part_send, part_recv, group_send, group_recv) = sems[:4]
        width = part.shape[-1]
        share = part.shape[2]
        quarter = tile.shape[2]

        def to_peer(step):
            peer = lax.rem(par + step, pars)
            return pltpu.make_async_remote_copy(
                src_ref=part.at[item, peer],
                dst_ref=met.at[item, step - 1],
                send_sem=part_send.at[item, step - 1],
                recv_sem=part_recv.at[item, step - 1],
                device_id=(lag, peer),
                device_id_type=MESH,
            )

        def among(source, target, send_sem, recv_sem, step, incoming):
            mate = lax.rem(member + step, members)
            place = mate if incoming else member
            return pltpu.make_async_remote_copy(
                src_ref=source.at[item, mate],
                dst_ref=target.at[item, place],
                send_sem=send_sem.at[item, mate],
                recv_sem=recv_sem.at[item, place],
                device_id=(base + mate, par),
                device_id_type=MESH,
            )

        gather = [
            functools.partial(among, tile_code, mates_code, sems[4], sems[5]),
            functools.partial(among, tile_scale, mates_scale, sems[6], sems[7]),
        ]
        give = [
            functools.partial(among, first_code, back_code, sems[8], sems[9]),
            functools.partial(among, first_scale, back_scale, sems[10], sems[11]),
        ]

        def receive(kinds, code, scale, target):
            for step in range(1, members):
                for kind in kinds:
                    kind(step, True).wait_recv()
                mate = lax.rem(member + step, members)
                target[item, mate] = decoded(code[item, mate], scale[item, mate])

        def to_group():
            return pltpu.make_async_remote_copy(
                src_ref=totals.at[item],
                dst_ref=ahead.at[item],
                send_sem=group_send.at[item],
                recv_sem=group_recv.at[item],
                device_id=(lag + members, par),
                device_id_type=MESH,
            )

        def multiply():
            product = lax.dot_general(
                prior[...], rows_ref[pl.ds(item * width, width), :], (((1,), (1,)), ((), ())),
                preferred_element_type=jnp.float32,
            )
            for owner in range(pars):
                part[item, owner] = product[owner * share:(owner + 1) * share]
            for step in range(1, pars):
                to_peer(step).start()

        def sum_peers():
            total = part[item, par]
            for step in range(1, pars):
                to_peer(step).wait_recv()
                total = total + met[item, step - 1]
            for owner in range(members):
                rows = total[owner * quarter:(owner + 1) * quarter]
                tile[item, owner] = rows
                tile_code[item, owner], tile_scale[item, owner] = coded(rows)
            for step in range(1, members):
                for kind in gather:
                    kind(step, False).start()
            mates[item, member] = tile[item, member]

        def sum_before():
            receive(gather, mates_code, mates_scale, mates)

            @pl.when(group == 0)
            def _():
                first[item, 0] = jnp.zeros_like(totals[item])

            @pl.when(group > 0)
            def _():
                to_group().wait_recv()
                first[item, 0] = ahead[item]

            before = first[item, 0]
            for mate in range(1, members):
                before = before + mates[item, mate - 1]
                first[item, mate] = before
            totals[item] = before + mates[item, members - 1]

            @pl.when(group < groups - 1)
            def _():
                to_group().start()

            for mate in range(members):
                first_code[item, mate], first_scale[item, mate] = coded(first[item, mate])
            for step in range(1, members):
                for kind in give:
                    kind(step, False).start()
            back[item, member] = first[item, member]

        def store():
            receive(give, back_code, back_scale, back)
            for owner in range(members):
                out_ref[0, owner * quarter:(owner + 1) * quarter, item * width:(item + 1) * width] = (
                    back[item, owner] + tile[item, owner]
                )

        def finish():
            for step in range(1, pars):
                to_peer(step).wait_send()
            for step in range(1, members):
                for kind in gather + give:
                    kind(step, False).wait_send()

            @pl.when(group < groups - 1)
            def _():
                to_group().wait_send()

        return multiply, sum_peers, sum_before, store, finish

    def arrive(item):
        @pl.when(lag < lags - 1)
        def _():
            shift(item).wait_recv()

        @pl.when(lag == lags - 1)
        def _():
            rows = pl.ds(item * span, span)
            coming[rows, :] = jnp.zeros((span, coming.shape[1]), coming.dtype)

    def depart(item):
        @pl.when(lag > 0)
        def _():
            shift(item).start()

    zeros = [
        stages_of(item, raw, zero_out, zero_buffers, zero_sems) for item in range(zero_items)
    ]
    ones = [
        stages_of(item, coming, one_out, one_buffers, one_sems) for item in range(one_items)
    ]
    lines = zeros + ones

    for item in range(one_items):
        depart(item)
    for load in loads:
        load.wait()
    for multiply, _, _, _, _ in zeros:
        multiply()
    for _, sum_peers, _, _, _ in zeros:
        sum_peers()
    for item, (multiply, sum_peers, _, _, _) in enumerate(ones):
        arrive(item)
        multiply()
        sum_peers()
    for _, _, sum_before, _, _ in lines:
        sum_before()
    for _, _, _, store, _ in lines:
        store()
    for _, _, _, _, finish in lines:
        finish()

    @pl.when(lag > 0)
    def _():
        for item in range(one_items):
            shift(item).wait_send()


def scratch_of(items, lags, pars, members, sensors):
    width, share = sensors // items, sensors // pars
    quarter = share // members
    f32 = jnp.float32
    buffers = [
        pltpu.VMEM((items, pars, share, width), f32),
        pltpu.VMEM((items, max(pars - 1, 1), share, width), f32),
        pltpu.VMEM((items, members, quarter, width), f32),
        pltpu.VMEM((items, members, quarter, width), f32),
        pltpu.VMEM((items, quarter, width), f32),
        pltpu.VMEM((items, quarter, width), f32),
        pltpu.VMEM((items, members, quarter, width), f32),
        pltpu.VMEM((items, members, quarter, width), f32),
    ]
    for _ in range(4):
        buffers.append(pltpu.VMEM((items, members, quarter, width), jnp.bfloat16))
        buffers.append(pltpu.VMEM((items, members, 1, width), f32))
    shapes = [(items, pars)] * 2 + [(items,)] * 2 + [(items, members)] * 8
    return tuple(buffers), tuple(pltpu.SemaphoreType.DMA(shape) for shape in shapes)


def solution(mesh):
    lags, pars = mesh.shape["lag"], mesh.shape["par"]

    def body(prior_rows, raw_rows):
        sensors, panel = prior_rows.shape[1:]
        share = sensors // pars
        members = group_size(lags, share)
        zero_items, one_items = 2, 4
        zero_buffers, zero_sems = scratch_of(zero_items, lags, pars, members, sensors)
        one_buffers, one_sems = scratch_of(one_items, lags, pars, members, sensors)
        out = jax.ShapeDtypeStruct((1, share, sensors), jnp.float32)
        return pl.pallas_call(
            functools.partial(kernel, lags, pars, members, zero_items, one_items),
            out_shape=(out, out),
            in_specs=[pl.BlockSpec(memory_space=pl.ANY)] * 2,
            out_specs=[pl.BlockSpec(memory_space=pltpu.VMEM)] * 2,
            scratch_shapes=[
                pltpu.VMEM((sensors, panel), jnp.bfloat16),
                pltpu.VMEM((sensors, panel), jnp.bfloat16),
                pltpu.VMEM((sensors, panel), jnp.bfloat16),
                zero_buffers,
                one_buffers,
                pltpu.SemaphoreType.DMA((2,)),
                pltpu.SemaphoreType.DMA((one_items,)),
                pltpu.SemaphoreType.DMA((one_items,)),
                zero_sems,
                one_sems,
            ],
            compiler_params=pltpu.CompilerParams(
                collective_id=0, has_side_effects=True, vmem_limit_bytes=52 * 2**20
            ),
            cost_estimate=pl.CostEstimate(
                flops=4 * sensors * sensors * panel,
                bytes_accessed=4 * sensors * panel + 8 * share * sensors,
                transcendentals=0,
            ),
        )(prior_rows, raw_rows)

    in_specs = (P("lag", None, "par"), P("lag", None, "par"))
    out_specs = (P("lag", "par", None), P("lag", "par", None))
    return jax.shard_map(body, mesh=mesh, in_specs=in_specs, out_specs=out_specs, check_vma=False)
```

```python
import functools

import jax
import jax.numpy as jnp
from jax import lax
from jax.experimental import pallas as pl
from jax.experimental.pallas import tpu as pltpu
from jax.sharding import PartitionSpec as P

MESH = pl.DeviceIdType.MESH
TOP = 240.0


def coded(values):
    scale = jnp.max(jnp.abs(values), axis=0, keepdims=True)
    power = values * (TOP / jnp.maximum(scale, 1e-36))
    negative = power < 0
    for _ in range(4):
        power = power * power
    return jnp.where(negative, -power, power).astype(jnp.bfloat16), scale * (1.0 / TOP)


def decoded(code, scale):
    code = code.astype(jnp.float32)
    root = jnp.maximum(jnp.abs(code), 2e-38)
    for _ in range(4):
        root = lax.rsqrt(root)
    root = root * scale
    return jnp.where(code == 0, 0.0, jnp.where(code < 0, -root, root))


def group_size(lags, rows):
    best = 1
    for size in range(1, lags + 1):
        if lags % size == 0 and size * size <= lags and rows % (16 * size) == 0:
            best = size
    return best


def kernel(
    lags, pars, members, zero_items, one_items,
    prior_hbm, raw_hbm, zero_out, one_out,
    prior, raw, coming,
    zero_buffers, one_buffers,
    load_sem, shift_send, shift_recv,
    zero_sems, one_sems,
):
    lag = lax.axis_index("lag")
    par = lax.axis_index("par")
    groups = lags // members
    group = lag // members
    member = lax.rem(lag, members)
    base = group * members

    loads = [
        pltpu.make_async_copy(prior_hbm.at[0], prior, load_sem.at[0]),
        pltpu.make_async_copy(raw_hbm.at[0], raw, load_sem.at[1]),
    ]
    for load in loads:
        load.start()

    barrier = pltpu.get_barrier_semaphore()

    def greet(other_lag, other_par):
        pl.semaphore_signal(barrier, inc=1, device_id=(other_lag, other_par), device_id_type=MESH)

    for step in range(1, pars):
        greet(lag, lax.rem(par + step, pars))
    for step in range(1, members):
        greet(base + lax.rem(member + step, members), par)
    met_by = (pars - 1) + (members - 1)
    for reach in [1] + [members * step for step in range(1, groups)]:
        @pl.when(lag >= reach)
        def _():
            greet(lag - reach, par)

        @pl.when(lag < lags - reach)
        def _():
            greet(lag + reach, par)

        met_by = met_by + (lag >= reach).astype(jnp.int32) + (lag < lags - reach).astype(jnp.int32)
    pl.semaphore_wait(barrier, met_by)

    span = raw.shape[0] // one_items

    def shift(item):
        rows = pl.ds(item * span, span)
        return pltpu.make_async_remote_copy(
            src_ref=raw_hbm.at[0, rows],
            dst_ref=coming.at[rows],
            send_sem=shift_send.at[item],
            recv_sem=shift_recv.at[item],
            device_id=(lag - 1, par),
            device_id_type=MESH,
        )

    def stages_of(item, rows_ref, out_ref, buffers, sems, reaches):
        (part, met, tile, mates, totals, ahead, first, back) = buffers[:8]
        (tile_code, tile_scale, mates_code, mates_scale) = buffers[8:12]
        (first_code, first_scale, back_code, back_scale) = buffers[12:]
        (part_send, part_recv, group_send, group_recv) = sems[:4]
        width = part.shape[-1]
        share = part.shape[2]
        quarter = tile.shape[2]

        def to_peer(step):
            peer = lax.rem(par + step, pars)
            return pltpu.make_async_remote_copy(
                src_ref=part.at[item, peer],
                dst_ref=met.at[item, step - 1],
                send_sem=part_send.at[item, step - 1],
                recv_sem=part_recv.at[item, step - 1],
                device_id=(lag, peer),
                device_id_type=MESH,
            )

        def among(source, target, send_sem, recv_sem, step, incoming):
            mate = lax.rem(member + step, members)
            place = mate if incoming else member
            return pltpu.make_async_remote_copy(
                src_ref=source.at[item, mate],
                dst_ref=target.at[item, place],
                send_sem=send_sem.at[item, mate],
                recv_sem=recv_sem.at[item, place],
                device_id=(base + mate, par),
                device_id_type=MESH,
            )

        gather = [
            functools.partial(among, tile_code, mates_code, sems[4], sems[5]),
            functools.partial(among, tile_scale, mates_scale, sems[6], sems[7]),
        ]
        give = [
            functools.partial(among, first_code, back_code, sems[8], sems[9]),
            functools.partial(among, first_scale, back_scale, sems[10], sems[11]),
        ]

        def receive(kinds, code, scale, target):
            for step in range(1, members):
                for kind in kinds:
                    kind(step, True).wait_recv()
                mate = lax.rem(member + step, members)
                target[item, mate] = decoded(code[item, mate], scale[item, mate])

        def to_group(reach):
            return pltpu.make_async_remote_copy(
                src_ref=totals.at[item],
                dst_ref=ahead.at[item, reach - 1],
                send_sem=group_send.at[item, reach - 1],
                recv_sem=group_recv.at[item, reach - 1],
                device_id=(lag + reach * members, par),
                device_id_type=MESH,
            )

        def multiply():
            product = lax.dot_general(
                prior[...], rows_ref[pl.ds(item * width, width), :], (((1,), (1,)), ((), ())),
                preferred_element_type=jnp.float32,
            )
            for owner in range(pars):
                part[item, owner] = product[owner * share:(owner + 1) * share]
            for step in range(1, pars):
                to_peer(step).start()

        def sum_peers():
            total = part[item, par]
            for step in range(1, pars):
                to_peer(step).wait_recv()
                total = total + met[item, step - 1]
            for owner in range(members):
                rows = total[owner * quarter:(owner + 1) * quarter]
                tile[item, owner] = rows
                tile_code[item, owner], tile_scale[item, owner] = coded(rows)
            for step in range(1, members):
                for kind in gather:
                    kind(step, False).start()
            mates[item, member] = tile[item, member]

        def sum_before():
            receive(gather, mates_code, mates_scale, mates)
            own = mates[item, 0]
            for mate in range(1, members):
                own = own + mates[item, mate]

            def send():
                for reach in reaches:
                    @pl.when(group + reach < groups)
                    def _():
                        to_group(reach).start()

            chained = len(reaches) == 1
            if not chained:
                totals[item] = own
                send()
            first[item, 0] = jnp.zeros_like(own)
            for reach in reaches:
                @pl.when(group >= reach)
                def _():
                    to_group(reach).wait_recv()
                    first[item, 0] += ahead[item, reach - 1]
            before = first[item, 0]
            if chained:
                totals[item] = before + own
                send()
            for mate in range(1, members):
                before = before + mates[item, mate - 1]
                first[item, mate] = before
            for mate in range(members):
                first_code[item, mate], first_scale[item, mate] = coded(first[item, mate])
            for step in range(1, members):
                for kind in give:
                    kind(step, False).start()
            back[item, member] = first[item, member]

        def store():
            receive(give, back_code, back_scale, back)
            for owner in range(members):
                out_ref[0, owner * quarter:(owner + 1) * quarter, item * width:(item + 1) * width] = (
                    back[item, owner] + tile[item, owner]
                )

        def finish():
            for step in range(1, pars):
                to_peer(step).wait_send()
            for step in range(1, members):
                for kind in gather + give:
                    kind(step, False).wait_send()

            for reach in reaches:
                @pl.when(group + reach < groups)
                def _():
                    to_group(reach).wait_send()

        return multiply, sum_peers, sum_before, store, finish

    def arrive(item):
        @pl.when(lag < lags - 1)
        def _():
            shift(item).wait_recv()

        @pl.when(lag == lags - 1)
        def _():
            rows = pl.ds(item * span, span)
            coming[rows, :] = jnp.zeros((span, coming.shape[1]), coming.dtype)

    def depart(item):
        @pl.when(lag > 0)
        def _():
            shift(item).start()

    zeros = [
        stages_of(item, raw, zero_out, zero_buffers, zero_sems, (1,)) for item in range(zero_items)
    ]
    ones = [
        stages_of(item, coming, one_out, one_buffers, one_sems, range(1, groups))
        for item in range(one_items)
    ]
    lines = zeros + ones
    last = one_items - 1

    def work_on(item):
        arrive(item)
        ones[item][0]()
        ones[item][1]()

    for item in range(last - 1):
        depart(item)
    for load in loads:
        load.wait()
    for multiply, _, _, _, _ in zeros:
        multiply()
    for _, sum_peers, _, _, _ in zeros:
        sum_peers()
    depart(last - 1)
    for item in range(last - 1):
        work_on(item)
    zeros[0][2]()
    depart(last)
    for _, _, sum_before, _, _ in zeros[1:]:
        sum_before()
    work_on(last - 1)
    for _, _, sum_before, _, _ in ones[:last - 1]:
        sum_before()
    zeros[0][3]()
    work_on(last)
    for _, _, sum_before, _, _ in ones[last - 1:]:
        sum_before()
    for _, _, _, store, _ in lines[1:]:
        store()
    for _, _, _, _, finish in lines:
        finish()

    @pl.when(lag > 0)
    def _():
        for item in range(one_items):
            shift(item).wait_send()


def scratch_of(items, lags, pars, members, reached, sensors):
    width, share = sensors // items, sensors // pars
    quarter = share // members
    f32 = jnp.float32
    buffers = [
        pltpu.VMEM((items, pars, share, width), f32),
        pltpu.VMEM((items, max(pars - 1, 1), share, width), f32),
        pltpu.VMEM((items, members, quarter, width), f32),
        pltpu.VMEM((items, members, quarter, width), f32),
        pltpu.VMEM((items, quarter, width), f32),
        pltpu.VMEM((items, reached, quarter, width), f32),
        pltpu.VMEM((items, members, quarter, width), f32),
        pltpu.VMEM((items, members, quarter, width), f32),
    ]
    for _ in range(4):
        buffers.append(pltpu.VMEM((items, members, quarter, width), jnp.bfloat16))
        buffers.append(pltpu.VMEM((items, members, 1, width), f32))
    shapes = [(items, pars)] * 2 + [(items, reached)] * 2 + [(items, members)] * 8
    return tuple(buffers), tuple(pltpu.SemaphoreType.DMA(shape) for shape in shapes)


def solution(mesh):
    lags, pars = mesh.shape["lag"], mesh.shape["par"]

    def body(prior_rows, raw_rows):
        sensors, panel = prior_rows.shape[1:]
        share = sensors // pars
        members = group_size(lags, share)
        zero_items, one_items = 2, 4
        zero_buffers, zero_sems = scratch_of(zero_items, lags, pars, members, 1, sensors)
        one_buffers, one_sems = scratch_of(one_items, lags, pars, members, max(lags // members - 1, 1), sensors)
        out = jax.ShapeDtypeStruct((1, share, sensors), jnp.float32)
        return pl.pallas_call(
            functools.partial(kernel, lags, pars, members, zero_items, one_items),
            out_shape=(out, out),
            in_specs=[pl.BlockSpec(memory_space=pl.ANY)] * 2,
            out_specs=[pl.BlockSpec(memory_space=pltpu.VMEM)] * 2,
            scratch_shapes=[
                pltpu.VMEM((sensors, panel), jnp.bfloat16),
                pltpu.VMEM((sensors, panel), jnp.bfloat16),
                pltpu.VMEM((sensors, panel), jnp.bfloat16),
                zero_buffers,
                one_buffers,
                pltpu.SemaphoreType.DMA((2,)),
                pltpu.SemaphoreType.DMA((one_items,)),
                pltpu.SemaphoreType.DMA((one_items,)),
                zero_sems,
                one_sems,
            ],
            compiler_params=pltpu.CompilerParams(
                collective_id=0, has_side_effects=True, vmem_limit_bytes=52 * 2**20
            ),
            cost_estimate=pl.CostEstimate(
                flops=4 * sensors * sensors * panel,
                bytes_accessed=4 * sensors * panel + 8 * share * sensors,
                transcendentals=0,
            ),
        )(prior_rows, raw_rows)

    in_specs = (P("lag", None, "par"), P("lag", None, "par"))
    out_specs = (P("lag", "par", None), P("lag", "par", None))
    return jax.shard_map(body, mesh=mesh, in_specs=in_specs, out_specs=out_specs, check_vma=False)
```

```python
import functools

import jax
import jax.numpy as jnp
from jax import lax
from jax.experimental import pallas as pl
from jax.experimental.pallas import tpu as pltpu
from jax.sharding import PartitionSpec as P

MESH = pl.DeviceIdType.MESH
TOP = 240.0


def coded(values):
    scale = jnp.max(jnp.abs(values), axis=0, keepdims=True)
    power = values * (TOP / jnp.maximum(scale, 1e-36))
    negative = power < 0
    for _ in range(4):
        power = power * power
    return jnp.where(negative, -power, power).astype(jnp.bfloat16), scale * (1.0 / TOP)


def decoded(code, scale):
    code = code.astype(jnp.float32)
    root = jnp.maximum(jnp.abs(code), 2e-38)
    for _ in range(4):
        root = lax.rsqrt(root)
    root = root * scale
    return jnp.where(code == 0, 0.0, jnp.where(code < 0, -root, root))


def group_size(lags, rows):
    best = 1
    for size in range(1, lags + 1):
        if lags % size == 0 and size * size <= lags and rows % (16 * size) == 0:
            best = size
    return best


def kernel(
    lags, pars, members, zero_items, one_items,
    prior_hbm, raw_hbm, zero_out, one_out,
    prior, raw, coming,
    zero_buffers, one_buffers,
    load_sem, shift_send, shift_recv,
    zero_sems, one_sems,
):
    lag = lax.axis_index("lag")
    par = lax.axis_index("par")
    groups = lags // members
    group = lag // members
    member = lax.rem(lag, members)
    base = group * members

    loads = [
        pltpu.make_async_copy(prior_hbm.at[0], prior, load_sem.at[0]),
        pltpu.make_async_copy(raw_hbm.at[0], raw, load_sem.at[1]),
    ]
    for load in loads:
        load.start()

    barrier = pltpu.get_barrier_semaphore()

    def greet(other_lag, other_par):
        pl.semaphore_signal(barrier, inc=1, device_id=(other_lag, other_par), device_id_type=MESH)

    for step in range(1, pars):
        greet(lag, lax.rem(par + step, pars))
    for step in range(1, members):
        greet(base + lax.rem(member + step, members), par)
    met_by = (pars - 1) + (members - 1)
    for reach in [1] + [members * step for step in range(1, groups)]:
        @pl.when(lag >= reach)
        def _():
            greet(lag - reach, par)

        @pl.when(lag < lags - reach)
        def _():
            greet(lag + reach, par)

        met_by = met_by + (lag >= reach).astype(jnp.int32) + (lag < lags - reach).astype(jnp.int32)
    pl.semaphore_wait(barrier, met_by)

    span = raw.shape[0] // one_items

    def shift(item):
        rows = pl.ds(item * span, span)
        return pltpu.make_async_remote_copy(
            src_ref=raw_hbm.at[0, rows],
            dst_ref=coming.at[rows],
            send_sem=shift_send.at[item],
            recv_sem=shift_recv.at[item],
            device_id=(lag - 1, par),
            device_id_type=MESH,
        )

    def stages_of(item, rows_ref, out_ref, buffers, sems, reaches):
        (part, met, tile, mates, totals, ahead, first, back) = buffers[:8]
        (tile_code, tile_scale, mates_code, mates_scale) = buffers[8:12]
        (first_code, first_scale, back_code, back_scale) = buffers[12:]
        (part_send, part_recv, group_send, group_recv) = sems[:4]
        width = part.shape[-1]
        share = part.shape[2]
        quarter = tile.shape[2]

        def to_peer(step):
            peer = lax.rem(par + step, pars)
            return pltpu.make_async_remote_copy(
                src_ref=part.at[item, peer],
                dst_ref=met.at[item, step - 1],
                send_sem=part_send.at[item, step - 1],
                recv_sem=part_recv.at[item, step - 1],
                device_id=(lag, peer),
                device_id_type=MESH,
            )

        def among(source, target, send_sem, recv_sem, step, incoming):
            mate = lax.rem(member + step, members)
            place = mate if incoming else member
            return pltpu.make_async_remote_copy(
                src_ref=source.at[item, mate],
                dst_ref=target.at[item, place],
                send_sem=send_sem.at[item, mate],
                recv_sem=recv_sem.at[item, place],
                device_id=(base + mate, par),
                device_id_type=MESH,
            )

        gather = [
            functools.partial(among, tile_code, mates_code, sems[4], sems[5]),
            functools.partial(among, tile_scale, mates_scale, sems[6], sems[7]),
        ]
        give = [
            functools.partial(among, first_code, back_code, sems[8], sems[9]),
            functools.partial(among, first_scale, back_scale, sems[10], sems[11]),
        ]

        def receive(kinds, code, scale, target):
            for step in range(1, members):
                for kind in kinds:
                    kind(step, True).wait_recv()
                mate = lax.rem(member + step, members)
                target[item, mate] = decoded(code[item, mate], scale[item, mate])

        def to_group(reach):
            return pltpu.make_async_remote_copy(
                src_ref=totals.at[item],
                dst_ref=ahead.at[item, reach - 1],
                send_sem=group_send.at[item, reach - 1],
                recv_sem=group_recv.at[item, reach - 1],
                device_id=(lag + reach * members, par),
                device_id_type=MESH,
            )

        def multiply():
            product = lax.dot_general(
                prior[...], rows_ref[pl.ds(item * width, width), :], (((1,), (1,)), ((), ())),
                preferred_element_type=jnp.float32,
            )
            for owner in range(pars):
                part[item, owner] = product[owner * share:(owner + 1) * share]
            for step in range(1, pars):
                to_peer(step).start()

        def sum_peers():
            total = part[item, par]
            for step in range(1, pars):
                to_peer(step).wait_recv()
                total = total + met[item, step - 1]
            for owner in range(members):
                rows = total[owner * quarter:(owner + 1) * quarter]
                tile[item, owner] = rows
                tile_code[item, owner], tile_scale[item, owner] = coded(rows)
            for step in range(1, members):
                for kind in gather:
                    kind(step, False).start()
            mates[item, member] = tile[item, member]

        def sum_before():
            receive(gather, mates_code, mates_scale, mates)
            own = mates[item, 0]
            for mate in range(1, members):
                own = own + mates[item, mate]

            def send():
                for reach in reaches:
                    @pl.when(group + reach < groups)
                    def _():
                        to_group(reach).start()

            chained = len(reaches) == 1
            if not chained:
                totals[item] = own
                send()
            first[item, 0] = jnp.zeros_like(own)
            for reach in reaches:
                @pl.when(group >= reach)
                def _():
                    to_group(reach).wait_recv()
                    first[item, 0] += ahead[item, reach - 1]
            before = first[item, 0]
            if chained:
                totals[item] = before + own
                send()
            for mate in range(1, members):
                before = before + mates[item, mate - 1]
                first[item, mate] = before
            for mate in range(members):
                first_code[item, mate], first_scale[item, mate] = coded(first[item, mate])
            for step in range(1, members):
                for kind in give:
                    kind(step, False).start()
            back[item, member] = first[item, member]

        def store():
            receive(give, back_code, back_scale, back)
            for owner in range(members):
                out_ref[0, owner * quarter:(owner + 1) * quarter, item * width:(item + 1) * width] = (
                    back[item, owner] + tile[item, owner]
                )

        def finish():
            for step in range(1, pars):
                to_peer(step).wait_send()
            for step in range(1, members):
                for kind in gather + give:
                    kind(step, False).wait_send()

            for reach in reaches:
                @pl.when(group + reach < groups)
                def _():
                    to_group(reach).wait_send()

        return multiply, sum_peers, sum_before, store, finish

    def arrive(item):
        @pl.when(lag < lags - 1)
        def _():
            shift(item).wait_recv()

        @pl.when(lag == lags - 1)
        def _():
            rows = pl.ds(item * span, span)
            coming[rows, :] = jnp.zeros((span, coming.shape[1]), coming.dtype)

    def depart(item):
        @pl.when(lag > 0)
        def _():
            shift(item).start()

    zeros = [
        stages_of(item, raw, zero_out, zero_buffers, zero_sems, (1,)) for item in range(zero_items)
    ]
    ones = [
        stages_of(item, coming, one_out, one_buffers, one_sems, range(1, groups))
        for item in range(one_items)
    ]
    lines = zeros + ones
    last = one_items - 1

    def work_on(item):
        ones[item][0]()
        ones[item][1]()

    for item in range(last - 1):
        depart(item)
    for load in loads:
        load.wait()
    for multiply, _, _, _, _ in zeros:
        multiply()
    for _, sum_peers, _, _, _ in zeros:
        sum_peers()
    depart(last - 1)
    for _, _, sum_before, _, _ in zeros:
        sum_before()
    for item in range(last - 1):
        arrive(item)
    depart(last)
    for item in range(last - 1):
        work_on(item)
    for _, _, _, store, _ in zeros:
        store()
    arrive(last - 1)
    work_on(last - 1)
    for _, _, sum_before, _, _ in ones[:last]:
        sum_before()
    for _, _, _, store, _ in ones[:last - 1]:
        store()
    arrive(last)
    work_on(last)
    ones[last][2]()
    ones[last - 1][3]()
    ones[last][3]()
    for _, _, _, _, finish in lines:
        finish()

    @pl.when(lag > 0)
    def _():
        for item in range(one_items):
            shift(item).wait_send()


def scratch_of(items, lags, pars, members, reached, sensors):
    width, share = sensors // items, sensors // pars
    quarter = share // members
    f32 = jnp.float32
    buffers = [
        pltpu.VMEM((items, pars, share, width), f32),
        pltpu.VMEM((items, max(pars - 1, 1), share, width), f32),
        pltpu.VMEM((items, members, quarter, width), f32),
        pltpu.VMEM((items, members, quarter, width), f32),
        pltpu.VMEM((items, quarter, width), f32),
        pltpu.VMEM((items, reached, quarter, width), f32),
        pltpu.VMEM((items, members, quarter, width), f32),
        pltpu.VMEM((items, members, quarter, width), f32),
    ]
    for _ in range(4):
        buffers.append(pltpu.VMEM((items, members, quarter, width), jnp.bfloat16))
        buffers.append(pltpu.VMEM((items, members, 1, width), f32))
    shapes = [(items, pars)] * 2 + [(items, reached)] * 2 + [(items, members)] * 8
    return tuple(buffers), tuple(pltpu.SemaphoreType.DMA(shape) for shape in shapes)


def solution(mesh):
    lags, pars = mesh.shape["lag"], mesh.shape["par"]

    def body(prior_rows, raw_rows):
        sensors, panel = prior_rows.shape[1:]
        share = sensors // pars
        members = group_size(lags, share)
        zero_items, one_items = 2, 4
        zero_buffers, zero_sems = scratch_of(zero_items, lags, pars, members, 1, sensors)
        one_buffers, one_sems = scratch_of(one_items, lags, pars, members, max(lags // members - 1, 1), sensors)
        out = jax.ShapeDtypeStruct((1, share, sensors), jnp.float32)
        return pl.pallas_call(
            functools.partial(kernel, lags, pars, members, zero_items, one_items),
            out_shape=(out, out),
            in_specs=[pl.BlockSpec(memory_space=pl.ANY)] * 2,
            out_specs=[pl.BlockSpec(memory_space=pltpu.VMEM)] * 2,
            scratch_shapes=[
                pltpu.VMEM((sensors, panel), jnp.bfloat16),
                pltpu.VMEM((sensors, panel), jnp.bfloat16),
                pltpu.VMEM((sensors, panel), jnp.bfloat16),
                zero_buffers,
                one_buffers,
                pltpu.SemaphoreType.DMA((2,)),
                pltpu.SemaphoreType.DMA((one_items,)),
                pltpu.SemaphoreType.DMA((one_items,)),
                zero_sems,
                one_sems,
            ],
            compiler_params=pltpu.CompilerParams(
                collective_id=0, has_side_effects=True, vmem_limit_bytes=52 * 2**20
            ),
            cost_estimate=pl.CostEstimate(
                flops=4 * sensors * sensors * panel,
                bytes_accessed=4 * sensors * panel + 8 * share * sensors,
                transcendentals=0,
            ),
        )(prior_rows, raw_rows)

    in_specs = (P("lag", None, "par"), P("lag", None, "par"))
    out_specs = (P("lag", "par", None), P("lag", "par", None))
    return jax.shard_map(body, mesh=mesh, in_specs=in_specs, out_specs=out_specs, check_vma=False)
```

```python
import functools

import jax
import jax.numpy as jnp
from jax import lax
from jax.experimental import pallas as pl
from jax.experimental.pallas import tpu as pltpu
from jax.sharding import PartitionSpec as P

MESH = pl.DeviceIdType.MESH
TOP = 240.0


def coded(values):
    scale = jnp.max(jnp.abs(values), axis=0, keepdims=True)
    power = values * (TOP / jnp.maximum(scale, 1e-36))
    negative = power < 0
    for _ in range(4):
        power = power * power
    return jnp.where(negative, -power, power).astype(jnp.bfloat16), scale * (1.0 / TOP)


def decoded(code, scale):
    code = code.astype(jnp.float32)
    root = jnp.maximum(jnp.abs(code), 2e-38)
    for _ in range(4):
        root = lax.rsqrt(root)
    root = root * scale
    return jnp.where(code == 0, 0.0, jnp.where(code < 0, -root, root))


def group_size(lags, rows):
    best = 1
    for size in range(1, lags + 1):
        if lags % size == 0 and size * size <= lags and rows % (16 * size) == 0:
            best = size
    return best


def kernel(
    lags, pars, members, zero_items, one_items,
    prior_hbm, raw_hbm, zero_out, one_out,
    prior, raw, coming,
    zero_buffers, one_buffers,
    load_sem, shift_send, shift_recv,
    zero_sems, one_sems,
):
    lag = lax.axis_index("lag")
    par = lax.axis_index("par")
    groups = lags // members
    group = lag // members
    member = lax.rem(lag, members)
    base = group * members

    loads = [
        pltpu.make_async_copy(prior_hbm.at[0], prior, load_sem.at[0]),
        pltpu.make_async_copy(raw_hbm.at[0], raw, load_sem.at[1]),
    ]
    for load in loads:
        load.start()

    barrier = pltpu.get_barrier_semaphore()

    def greet(other_lag, other_par):
        pl.semaphore_signal(barrier, inc=1, device_id=(other_lag, other_par), device_id_type=MESH)

    for step in range(1, pars):
        greet(lag, lax.rem(par + step, pars))
    for step in range(1, members):
        greet(base + lax.rem(member + step, members), par)
    met_by = (pars - 1) + (members - 1)
    for reach in (1, members):
        @pl.when(lag >= reach)
        def _():
            greet(lag - reach, par)

        @pl.when(lag < lags - reach)
        def _():
            greet(lag + reach, par)

        met_by = met_by + (lag >= reach).astype(jnp.int32) + (lag < lags - reach).astype(jnp.int32)
    pl.semaphore_wait(barrier, met_by)

    span = raw.shape[0] // one_items

    def shift(item):
        rows = pl.ds(item * span, span)
        return pltpu.make_async_remote_copy(
            src_ref=raw_hbm.at[0, rows],
            dst_ref=coming.at[rows],
            send_sem=shift_send.at[item],
            recv_sem=shift_recv.at[item],
            device_id=(lag - 1, par),
            device_id_type=MESH,
        )

    def stages_of(item, rows_ref, out_ref, buffers, sems):
        (part, met, tile, mates, totals, ahead, first, back) = buffers[:8]
        (tile_code, tile_scale, mates_code, mates_scale) = buffers[8:12]
        (first_code, first_scale, back_code, back_scale) = buffers[12:]
        (part_send, part_recv, group_send, group_recv) = sems[:4]
        width = part.shape[-1]
        share = part.shape[2]
        quarter = tile.shape[2]

        def to_peer(step):
            peer = lax.rem(par + step, pars)
            return pltpu.make_async_remote_copy(
                src_ref=part.at[item, peer],
                dst_ref=met.at[item, step - 1],
                send_sem=part_send.at[item, step - 1],
                recv_sem=part_recv.at[item, step - 1],
                device_id=(lag, peer),
                device_id_type=MESH,
            )

        def among(source, target, send_sem, recv_sem, step, incoming):
            mate = lax.rem(member + step, members)
            place = mate if incoming else member
            return pltpu.make_async_remote_copy(
                src_ref=source.at[item, mate],
                dst_ref=target.at[item, place],
                send_sem=send_sem.at[item, mate],
                recv_sem=recv_sem.at[item, place],
                device_id=(base + mate, par),
                device_id_type=MESH,
            )

        gather = [
            functools.partial(among, tile_code, mates_code, sems[4], sems[5]),
            functools.partial(among, tile_scale, mates_scale, sems[6], sems[7]),
        ]
        give = [
            functools.partial(among, first_code, back_code, sems[8], sems[9]),
            functools.partial(among, first_scale, back_scale, sems[10], sems[11]),
        ]

        def receive(kinds, code, scale, target):
            for step in range(1, members):
                for kind in kinds:
                    kind(step, True).wait_recv()
                mate = lax.rem(member + step, members)
                target[item, mate] = decoded(code[item, mate], scale[item, mate])

        def to_group():
            return pltpu.make_async_remote_copy(
                src_ref=totals.at[item],
                dst_ref=ahead.at[item],
                send_sem=group_send.at[item],
                recv_sem=group_recv.at[item],
                device_id=(lag + members, par),
                device_id_type=MESH,
            )

        def multiply():
            product = lax.dot_general(
                prior[...], rows_ref[pl.ds(item * width, width), :], (((1,), (1,)), ((), ())),
                preferred_element_type=jnp.float32,
            )
            for owner in range(pars):
                part[item, owner] = product[owner * share:(owner + 1) * share]
            for step in range(1, pars):
                to_peer(step).start()

        def sum_peers():
            total = part[item, par]
            for step in range(1, pars):
                to_peer(step).wait_recv()
                total = total + met[item, step - 1]
            for owner in range(members):
                rows = total[owner * quarter:(owner + 1) * quarter]
                tile[item, owner] = rows
                tile_code[item, owner], tile_scale[item, owner] = coded(rows)
            for step in range(1, members):
                for kind in gather:
                    kind(step, False).start()
            mates[item, member] = tile[item, member]

        def sum_before():
            receive(gather, mates_code, mates_scale, mates)

            @pl.when(group == 0)
            def _():
                first[item, 0] = jnp.zeros_like(totals[item])

            @pl.when(group > 0)
            def _():
                to_group().wait_recv()
                first[item, 0] = ahead[item]

            before = first[item, 0]
            for mate in range(1, members):
                before = before + mates[item, mate - 1]
                first[item, mate] = before
            totals[item] = before + mates[item, members - 1]

            @pl.when(group < groups - 1)
            def _():
                to_group().start()

            for mate in range(members):
                first_code[item, mate], first_scale[item, mate] = coded(first[item, mate])
            for step in range(1, members):
                for kind in give:
                    kind(step, False).start()
            back[item, member] = first[item, member]

        def store():
            receive(give, back_code, back_scale, back)
            for owner in range(members):
                out_ref[0, owner * quarter:(owner + 1) * quarter, item * width:(item + 1) * width] = (
                    back[item, owner] + tile[item, owner]
                )

        def finish():
            for step in range(1, pars):
                to_peer(step).wait_send()
            for step in range(1, members):
                for kind in gather + give:
                    kind(step, False).wait_send()

            @pl.when(group < groups - 1)
            def _():
                to_group().wait_send()

        return multiply, sum_peers, sum_before, store, finish

    def arrive(item):
        @pl.when(lag < lags - 1)
        def _():
            shift(item).wait_recv()

        @pl.when(lag == lags - 1)
        def _():
            rows = pl.ds(item * span, span)
            coming[rows, :] = jnp.zeros((span, coming.shape[1]), coming.dtype)

    def depart(item):
        @pl.when(lag > 0)
        def _():
            shift(item).start()

    zeros = [
        stages_of(item, raw, zero_out, zero_buffers, zero_sems) for item in range(zero_items)
    ]
    ones = [
        stages_of(item, coming, one_out, one_buffers, one_sems) for item in range(one_items)
    ]
    lines = zeros + ones

    last = one_items - 1
    for item in range(last - 1):
        depart(item)
    for load in loads:
        load.wait()
    for multiply, _, _, _, _ in zeros:
        multiply()
    depart(last - 1)
    for item in range(last - 1):
        arrive(item)
        ones[item][0]()
    for _, sum_peers, _, _, _ in zeros:
        sum_peers()
    depart(last)
    arrive(last - 1)
    ones[last - 1][0]()
    for _, sum_peers, _, _, _ in ones[:last - 1]:
        sum_peers()
    arrive(last)
    ones[last][0]()
    for _, sum_peers, _, _, _ in ones[last - 1:]:
        sum_peers()
    for _, _, sum_before, _, _ in lines:
        sum_before()
    for _, _, _, store, _ in lines:
        store()
    for _, _, _, _, finish in lines:
        finish()

    @pl.when(lag > 0)
    def _():
        for item in range(one_items):
            shift(item).wait_send()


def scratch_of(items, lags, pars, members, sensors):
    width, share = sensors // items, sensors // pars
    quarter = share // members
    f32 = jnp.float32
    buffers = [
        pltpu.VMEM((items, pars, share, width), f32),
        pltpu.VMEM((items, max(pars - 1, 1), share, width), f32),
        pltpu.VMEM((items, members, quarter, width), f32),
        pltpu.VMEM((items, members, quarter, width), f32),
        pltpu.VMEM((items, quarter, width), f32),
        pltpu.VMEM((items, quarter, width), f32),
        pltpu.VMEM((items, members, quarter, width), f32),
        pltpu.VMEM((items, members, quarter, width), f32),
    ]
    for _ in range(4):
        buffers.append(pltpu.VMEM((items, members, quarter, width), jnp.bfloat16))
        buffers.append(pltpu.VMEM((items, members, 1, width), f32))
    shapes = [(items, pars)] * 2 + [(items,)] * 2 + [(items, members)] * 8
    return tuple(buffers), tuple(pltpu.SemaphoreType.DMA(shape) for shape in shapes)


def solution(mesh):
    lags, pars = mesh.shape["lag"], mesh.shape["par"]

    def body(prior_rows, raw_rows):
        sensors, panel = prior_rows.shape[1:]
        share = sensors // pars
        members = group_size(lags, share)
        zero_items, one_items = 2, 4
        zero_buffers, zero_sems = scratch_of(zero_items, lags, pars, members, sensors)
        one_buffers, one_sems = scratch_of(one_items, lags, pars, members, sensors)
        out = jax.ShapeDtypeStruct((1, share, sensors), jnp.float32)
        return pl.pallas_call(
            functools.partial(kernel, lags, pars, members, zero_items, one_items),
            out_shape=(out, out),
            in_specs=[pl.BlockSpec(memory_space=pl.ANY)] * 2,
            out_specs=[pl.BlockSpec(memory_space=pltpu.VMEM)] * 2,
            scratch_shapes=[
                pltpu.VMEM((sensors, panel), jnp.bfloat16),
                pltpu.VMEM((sensors, panel), jnp.bfloat16),
                pltpu.VMEM((sensors, panel), jnp.bfloat16),
                zero_buffers,
                one_buffers,
                pltpu.SemaphoreType.DMA((2,)),
                pltpu.SemaphoreType.DMA((one_items,)),
                pltpu.SemaphoreType.DMA((one_items,)),
                zero_sems,
                one_sems,
            ],
            compiler_params=pltpu.CompilerParams(
                collective_id=0, has_side_effects=True, vmem_limit_bytes=52 * 2**20
            ),
            cost_estimate=pl.CostEstimate(
                flops=4 * sensors * sensors * panel,
                bytes_accessed=4 * sensors * panel + 8 * share * sensors,
                transcendentals=0,
            ),
        )(prior_rows, raw_rows)

    in_specs = (P("lag", None, "par"), P("lag", None, "par"))
    out_specs = (P("lag", "par", None), P("lag", "par", None))
    return jax.shard_map(body, mesh=mesh, in_specs=in_specs, out_specs=out_specs, check_vma=False)
```

```python
import functools

import jax
import jax.numpy as jnp
from jax import lax
from jax.experimental import pallas as pl
from jax.experimental.pallas import tpu as pltpu
from jax.sharding import PartitionSpec as P

MESH = pl.DeviceIdType.MESH
TOP = 240.0


def coded(values):
    scale = jnp.max(jnp.abs(values), axis=0, keepdims=True)
    power = values * (TOP / jnp.maximum(scale, 1e-36))
    negative = power < 0
    for _ in range(4):
        power = power * power
    return jnp.where(negative, -power, power).astype(jnp.bfloat16), scale * (1.0 / TOP)


def decoded(code, scale):
    code = code.astype(jnp.float32)
    root = jnp.maximum(jnp.abs(code), 2e-38)
    for _ in range(4):
        root = lax.rsqrt(root)
    root = root * scale
    return jnp.where(code == 0, 0.0, jnp.where(code < 0, -root, root))


def group_size(lags, rows):
    best = 1
    for size in range(1, lags + 1):
        if lags % size == 0 and size * size <= lags and rows % (16 * size) == 0:
            best = size
    return best


def kernel(
    lags, pars, members, zero_items, one_items,
    prior_hbm, raw_hbm, zero_out, one_out,
    prior, raw, coming,
    zero_buffers, one_buffers,
    load_sem, shift_send, shift_recv,
    zero_sems, one_sems,
):
    lag = lax.axis_index("lag")
    par = lax.axis_index("par")
    groups = lags // members
    group = lag // members
    member = lax.rem(lag, members)
    base = group * members

    loads = [
        pltpu.make_async_copy(prior_hbm.at[0], prior, load_sem.at[0]),
        pltpu.make_async_copy(raw_hbm.at[0], raw, load_sem.at[1]),
    ]
    for load in loads:
        load.start()

    barrier = pltpu.get_barrier_semaphore()

    def greet(other_lag, other_par):
        pl.semaphore_signal(barrier, inc=1, device_id=(other_lag, other_par), device_id_type=MESH)

    for step in range(1, pars):
        greet(lag, lax.rem(par + step, pars))
    for step in range(1, members):
        greet(base + lax.rem(member + step, members), par)
    met_by = (pars - 1) + (members - 1)
    for reach in (1, members):
        @pl.when(lag >= reach)
        def _():
            greet(lag - reach, par)

        @pl.when(lag < lags - reach)
        def _():
            greet(lag + reach, par)

        met_by = met_by + (lag >= reach).astype(jnp.int32) + (lag < lags - reach).astype(jnp.int32)
    pl.semaphore_wait(barrier, met_by)

    span = raw.shape[0] // one_items

    def shift(item):
        rows = pl.ds(item * span, span)
        return pltpu.make_async_remote_copy(
            src_ref=raw_hbm.at[0, rows],
            dst_ref=coming.at[rows],
            send_sem=shift_send.at[item],
            recv_sem=shift_recv.at[item],
            device_id=(lag - 1, par),
            device_id_type=MESH,
        )

    def stages_of(item, rows_ref, out_ref, buffers, sems):
        (part, met, tile, mates, totals, ahead, first, back) = buffers[:8]
        (tile_code, tile_scale, mates_code, mates_scale) = buffers[8:12]
        (first_code, first_scale, back_code, back_scale) = buffers[12:]
        (part_send, part_recv, group_send, group_recv) = sems[:4]
        width = part.shape[-1]
        share = part.shape[2]
        quarter = tile.shape[2]

        def to_peer(step):
            peer = lax.rem(par + step, pars)
            return pltpu.make_async_remote_copy(
                src_ref=part.at[item, peer],
                dst_ref=met.at[item, step - 1],
                send_sem=part_send.at[item, step - 1],
                recv_sem=part_recv.at[item, step - 1],
                device_id=(lag, peer),
                device_id_type=MESH,
            )

        def among(source, target, send_sem, recv_sem, step, incoming):
            mate = lax.rem(member + step, members)
            place = mate if incoming else member
            return pltpu.make_async_remote_copy(
                src_ref=source.at[item, mate],
                dst_ref=target.at[item, place],
                send_sem=send_sem.at[item, mate],
                recv_sem=recv_sem.at[item, place],
                device_id=(base + mate, par),
                device_id_type=MESH,
            )

        gather = [
            functools.partial(among, tile_code, mates_code, sems[4], sems[5]),
            functools.partial(among, tile_scale, mates_scale, sems[6], sems[7]),
        ]
        give = [
            functools.partial(among, first_code, back_code, sems[8], sems[9]),
            functools.partial(among, first_scale, back_scale, sems[10], sems[11]),
        ]

        def receive(kinds, code, scale, target):
            for step in range(1, members):
                for kind in kinds:
                    kind(step, True).wait_recv()
                mate = lax.rem(member + step, members)
                target[item, mate] = decoded(code[item, mate], scale[item, mate])

        def to_group():
            return pltpu.make_async_remote_copy(
                src_ref=totals.at[item],
                dst_ref=ahead.at[item],
                send_sem=group_send.at[item],
                recv_sem=group_recv.at[item],
                device_id=(lag + members, par),
                device_id_type=MESH,
            )

        def multiply():
            product = lax.dot_general(
                prior[...], rows_ref[pl.ds(item * width, width), :], (((1,), (1,)), ((), ())),
                preferred_element_type=jnp.float32,
            )
            for owner in range(pars):
                part[item, owner] = product[owner * share:(owner + 1) * share]
            for step in range(1, pars):
                to_peer(step).start()

        def sum_peers():
            total = part[item, par]
            for step in range(1, pars):
                to_peer(step).wait_recv()
                total = total + met[item, step - 1]
            for owner in range(members):
                rows = total[owner * quarter:(owner + 1) * quarter]
                tile[item, owner] = rows
                tile_code[item, owner], tile_scale[item, owner] = coded(rows)
            for step in range(1, members):
                for kind in gather:
                    kind(step, False).start()
            mates[item, member] = tile[item, member]

        def sum_before():
            receive(gather, mates_code, mates_scale, mates)

            @pl.when(group == 0)
            def _():
                first[item, 0] = jnp.zeros_like(totals[item])

            @pl.when(group > 0)
            def _():
                to_group().wait_recv()
                first[item, 0] = ahead[item]

            before = first[item, 0]
            for mate in range(1, members):
                before = before + mates[item, mate - 1]
                first[item, mate] = before
            totals[item] = before + mates[item, members - 1]

            @pl.when(group < groups - 1)
            def _():
                to_group().start()

            for mate in range(members):
                first_code[item, mate], first_scale[item, mate] = coded(first[item, mate])
            for step in range(1, members):
                for kind in give:
                    kind(step, False).start()
            back[item, member] = first[item, member]

        def store():
            receive(give, back_code, back_scale, back)
            for owner in range(members):
                out_ref[0, owner * quarter:(owner + 1) * quarter, item * width:(item + 1) * width] = (
                    back[item, owner] + tile[item, owner]
                )

        def finish():
            for step in range(1, pars):
                to_peer(step).wait_send()
            for step in range(1, members):
                for kind in gather + give:
                    kind(step, False).wait_send()

            @pl.when(group < groups - 1)
            def _():
                to_group().wait_send()

        return multiply, sum_peers, sum_before, store, finish

    def arrive(item):
        @pl.when(lag < lags - 1)
        def _():
            shift(item).wait_recv()

        @pl.when(lag == lags - 1)
        def _():
            rows = pl.ds(item * span, span)
            coming[rows, :] = jnp.zeros((span, coming.shape[1]), coming.dtype)

    def depart(item):
        @pl.when(lag > 0)
        def _():
            shift(item).start()

    zeros = [
        stages_of(item, raw, zero_out, zero_buffers, zero_sems) for item in range(zero_items)
    ]
    ones = [
        stages_of(item, coming, one_out, one_buffers, one_sems) for item in range(one_items)
    ]
    lines = zeros + ones

    for item in range(one_items):
        depart(item)
    for load in loads:
        load.wait()
    for multiply, _, _, _, _ in zeros:
        multiply()
    for item, (multiply, _, _, _, _) in enumerate(ones):
        arrive(item)
        multiply()
    for _, sum_peers, _, _, _ in lines:
        sum_peers()
    for _, _, sum_before, _, _ in lines:
        sum_before()
    for _, _, _, store, _ in lines:
        store()
    for _, _, _, _, finish in lines:
        finish()

    @pl.when(lag > 0)
    def _():
        for item in range(one_items):
            shift(item).wait_send()


def scratch_of(items, lags, pars, members, sensors):
    width, share = sensors // items, sensors // pars
    quarter = share // members
    f32 = jnp.float32
    buffers = [
        pltpu.VMEM((items, pars, share, width), f32),
        pltpu.VMEM((items, max(pars - 1, 1), share, width), f32),
        pltpu.VMEM((items, members, quarter, width), f32),
        pltpu.VMEM((items, members, quarter, width), f32),
        pltpu.VMEM((items, quarter, width), f32),
        pltpu.VMEM((items, quarter, width), f32),
        pltpu.VMEM((items, members, quarter, width), f32),
        pltpu.VMEM((items, members, quarter, width), f32),
    ]
    for _ in range(4):
        buffers.append(pltpu.VMEM((items, members, quarter, width), jnp.bfloat16))
        buffers.append(pltpu.VMEM((items, members, 1, width), f32))
    shapes = [(items, pars)] * 2 + [(items,)] * 2 + [(items, members)] * 8
    return tuple(buffers), tuple(pltpu.SemaphoreType.DMA(shape) for shape in shapes)


def solution(mesh):
    lags, pars = mesh.shape["lag"], mesh.shape["par"]

    def body(prior_rows, raw_rows):
        sensors, panel = prior_rows.shape[1:]
        share = sensors // pars
        members = group_size(lags, share)
        zero_items, one_items = 2, 4
        zero_buffers, zero_sems = scratch_of(zero_items, lags, pars, members, sensors)
        one_buffers, one_sems = scratch_of(one_items, lags, pars, members, sensors)
        out = jax.ShapeDtypeStruct((1, share, sensors), jnp.float32)
        return pl.pallas_call(
            functools.partial(kernel, lags, pars, members, zero_items, one_items),
            out_shape=(out, out),
            in_specs=[pl.BlockSpec(memory_space=pl.ANY)] * 2,
            out_specs=[pl.BlockSpec(memory_space=pltpu.VMEM)] * 2,
            scratch_shapes=[
                pltpu.VMEM((sensors, panel), jnp.bfloat16),
                pltpu.VMEM((sensors, panel), jnp.bfloat16),
                pltpu.VMEM((sensors, panel), jnp.bfloat16),
                zero_buffers,
                one_buffers,
                pltpu.SemaphoreType.DMA((2,)),
                pltpu.SemaphoreType.DMA((one_items,)),
                pltpu.SemaphoreType.DMA((one_items,)),
                zero_sems,
                one_sems,
            ],
            compiler_params=pltpu.CompilerParams(
                collective_id=0, has_side_effects=True, vmem_limit_bytes=52 * 2**20
            ),
            cost_estimate=pl.CostEstimate(
                flops=4 * sensors * sensors * panel,
                bytes_accessed=4 * sensors * panel + 8 * share * sensors,
                transcendentals=0,
            ),
        )(prior_rows, raw_rows)

    in_specs = (P("lag", None, "par"), P("lag", None, "par"))
    out_specs = (P("lag", "par", None), P("lag", "par", None))
    return jax.shard_map(body, mesh=mesh, in_specs=in_specs, out_specs=out_specs, check_vma=False)
```

```python
import functools

import jax
import jax.numpy as jnp
from jax import lax
from jax.experimental import pallas as pl
from jax.experimental.pallas import tpu as pltpu
from jax.sharding import PartitionSpec as P

MESH = pl.DeviceIdType.MESH
TOP = 240.0


def coded(values):
    scale = jnp.max(jnp.abs(values), axis=0, keepdims=True)
    power = values * (TOP / jnp.maximum(scale, 1e-36))
    negative = power < 0
    for _ in range(4):
        power = power * power
    return jnp.where(negative, -power, power).astype(jnp.bfloat16), scale * (1.0 / TOP)


def decoded(code, scale):
    code = code.astype(jnp.float32)
    root = jnp.maximum(jnp.abs(code), 2e-38)
    for _ in range(4):
        root = lax.rsqrt(root)
    root = root * scale
    return jnp.where(code == 0, 0.0, jnp.where(code < 0, -root, root))


def group_size(lags, rows):
    best = 1
    for size in range(1, lags + 1):
        if lags % size == 0 and size * size <= lags and rows % (16 * size) == 0:
            best = size
    return best


def kernel(
    lags, pars, members, zero_items, one_items,
    prior_hbm, raw_hbm, zero_out, one_out,
    prior, raw, coming,
    zero_buffers, one_buffers,
    load_sem, shift_send, shift_recv,
    zero_sems, one_sems,
):
    lag = lax.axis_index("lag")
    par = lax.axis_index("par")
    groups = lags // members
    group = lag // members
    member = lax.rem(lag, members)
    base = group * members

    loads = [
        pltpu.make_async_copy(prior_hbm.at[0], prior, load_sem.at[0]),
        pltpu.make_async_copy(raw_hbm.at[0], raw, load_sem.at[1]),
    ]
    for load in loads:
        load.start()

    barrier = pltpu.get_barrier_semaphore()

    def greet(other_lag, other_par):
        pl.semaphore_signal(barrier, inc=1, device_id=(other_lag, other_par), device_id_type=MESH)

    for step in range(1, pars):
        greet(lag, lax.rem(par + step, pars))
    for step in range(1, members):
        greet(base + lax.rem(member + step, members), par)
    met_by = (pars - 1) + (members - 1)
    for reach in (1, members):
        @pl.when(lag >= reach)
        def _():
            greet(lag - reach, par)

        @pl.when(lag < lags - reach)
        def _():
            greet(lag + reach, par)

        met_by = met_by + (lag >= reach).astype(jnp.int32) + (lag < lags - reach).astype(jnp.int32)
    pl.semaphore_wait(barrier, met_by)

    span = raw.shape[0] // one_items

    def shift(item):
        rows = pl.ds(item * span, span)
        return pltpu.make_async_remote_copy(
            src_ref=raw_hbm.at[0, rows],
            dst_ref=coming.at[rows],
            send_sem=shift_send.at[item],
            recv_sem=shift_recv.at[item],
            device_id=(lag - 1, par),
            device_id_type=MESH,
        )

    def stages_of(item, rows_ref, out_ref, buffers, sems):
        (part, met, tile, mates, totals, ahead, first, back) = buffers[:8]
        (tile_code, tile_scale, mates_code, mates_scale) = buffers[8:12]
        (first_code, first_scale, back_code, back_scale) = buffers[12:]
        (part_send, part_recv, group_send, group_recv) = sems[:4]
        width = part.shape[-1]
        share = part.shape[2]
        quarter = tile.shape[2]

        def to_peer(step):
            peer = lax.rem(par + step, pars)
            return pltpu.make_async_remote_copy(
                src_ref=part.at[item, peer],
                dst_ref=met.at[item, step - 1],
                send_sem=part_send.at[item, step - 1],
                recv_sem=part_recv.at[item, step - 1],
                device_id=(lag, peer),
                device_id_type=MESH,
            )

        def among(source, target, send_sem, recv_sem, step, incoming):
            mate = lax.rem(member + step, members)
            place = mate if incoming else member
            return pltpu.make_async_remote_copy(
                src_ref=source.at[item, mate],
                dst_ref=target.at[item, place],
                send_sem=send_sem.at[item, mate],
                recv_sem=recv_sem.at[item, place],
                device_id=(base + mate, par),
                device_id_type=MESH,
            )

        gather = [
            functools.partial(among, tile_code, mates_code, sems[4], sems[5]),
            functools.partial(among, tile_scale, mates_scale, sems[6], sems[7]),
        ]
        give = [
            functools.partial(among, first_code, back_code, sems[8], sems[9]),
            functools.partial(among, first_scale, back_scale, sems[10], sems[11]),
        ]

        def receive(kinds, code, scale, target):
            for step in range(1, members):
                for kind in kinds:
                    kind(step, True).wait_recv()
                mate = lax.rem(member + step, members)
                target[item, mate] = decoded(code[item, mate], scale[item, mate])

        def to_group():
            return pltpu.make_async_remote_copy(
                src_ref=totals.at[item],
                dst_ref=ahead.at[item],
                send_sem=group_send.at[item],
                recv_sem=group_recv.at[item],
                device_id=(lag + members, par),
                device_id_type=MESH,
            )

        def multiply():
            product = lax.dot_general(
                prior[...], rows_ref[pl.ds(item * width, width), :], (((1,), (1,)), ((), ())),
                preferred_element_type=jnp.float32,
            )
            for owner in range(pars):
                part[item, owner] = product[owner * share:(owner + 1) * share]
            for step in range(1, pars):
                to_peer(step).start()

        def sum_peers():
            total = part[item, par]
            for step in range(1, pars):
                to_peer(step).wait_recv()
                total = total + met[item, step - 1]
            for owner in range(members):
                rows = total[owner * quarter:(owner + 1) * quarter]
                tile[item, owner] = rows
                tile_code[item, owner], tile_scale[item, owner] = coded(rows)
            for step in range(1, members):
                for kind in gather:
                    kind(step, False).start()
            mates[item, member] = tile[item, member]

        def gather_tiles():
            receive(gather, mates_code, mates_scale, mates)

        def sum_groups():
            own = mates[item, 0]
            for mate in range(1, members):
                own = own + mates[item, mate]

            @pl.when(group == 0)
            def _():
                first[item, 0] = jnp.zeros_like(own)

            @pl.when(group > 0)
            def _():
                to_group().wait_recv()
                first[item, 0] = ahead[item]

            totals[item] = first[item, 0] + own

            @pl.when(group < groups - 1)
            def _():
                to_group().start()

        def sum_before():
            before = first[item, 0]
            for mate in range(1, members):
                before = before + mates[item, mate - 1]
                first[item, mate] = before
            for mate in range(members):
                first_code[item, mate], first_scale[item, mate] = coded(first[item, mate])
            for step in range(1, members):
                for kind in give:
                    kind(step, False).start()
            back[item, member] = first[item, member]

        def store():
            receive(give, back_code, back_scale, back)
            for owner in range(members):
                out_ref[0, owner * quarter:(owner + 1) * quarter, item * width:(item + 1) * width] = (
                    back[item, owner] + tile[item, owner]
                )

        def finish():
            for step in range(1, pars):
                to_peer(step).wait_send()
            for step in range(1, members):
                for kind in gather + give:
                    kind(step, False).wait_send()

            @pl.when(group < groups - 1)
            def _():
                to_group().wait_send()

        return multiply, sum_peers, (gather_tiles, sum_groups, sum_before), store, finish

    def arrive(item):
        @pl.when(lag < lags - 1)
        def _():
            shift(item).wait_recv()

        @pl.when(lag == lags - 1)
        def _():
            rows = pl.ds(item * span, span)
            coming[rows, :] = jnp.zeros((span, coming.shape[1]), coming.dtype)

    def depart(item):
        @pl.when(lag > 0)
        def _():
            shift(item).start()

    zeros = [
        stages_of(item, raw, zero_out, zero_buffers, zero_sems) for item in range(zero_items)
    ]
    ones = [
        stages_of(item, coming, one_out, one_buffers, one_sems) for item in range(one_items)
    ]
    lines = zeros + ones

    for item in range(one_items):
        depart(item)
    for load in loads:
        load.wait()
    for multiply, _, _, _, _ in zeros:
        multiply()
    for _, sum_peers, _, _, _ in zeros:
        sum_peers()
    for item, (multiply, sum_peers, _, _, _) in enumerate(ones):
        arrive(item)
        multiply()
        sum_peers()
    for stage in range(3):
        for _, _, prefix, _, _ in lines:
            prefix[stage]()
    for _, _, _, store, _ in lines:
        store()
    for _, _, _, _, finish in lines:
        finish()

    @pl.when(lag > 0)
    def _():
        for item in range(one_items):
            shift(item).wait_send()


def scratch_of(items, lags, pars, members, sensors):
    width, share = sensors // items, sensors // pars
    quarter = share // members
    f32 = jnp.float32
    buffers = [
        pltpu.VMEM((items, pars, share, width), f32),
        pltpu.VMEM((items, max(pars - 1, 1), share, width), f32),
        pltpu.VMEM((items, members, quarter, width), f32),
        pltpu.VMEM((items, members, quarter, width), f32),
        pltpu.VMEM((items, quarter, width), f32),
        pltpu.VMEM((items, quarter, width), f32),
        pltpu.VMEM((items, members, quarter, width), f32),
        pltpu.VMEM((items, members, quarter, width), f32),
    ]
    for _ in range(4):
        buffers.append(pltpu.VMEM((items, members, quarter, width), jnp.bfloat16))
        buffers.append(pltpu.VMEM((items, members, 1, width), f32))
    shapes = [(items, pars)] * 2 + [(items,)] * 2 + [(items, members)] * 8
    return tuple(buffers), tuple(pltpu.SemaphoreType.DMA(shape) for shape in shapes)


def solution(mesh):
    lags, pars = mesh.shape["lag"], mesh.shape["par"]

    def body(prior_rows, raw_rows):
        sensors, panel = prior_rows.shape[1:]
        share = sensors // pars
        members = group_size(lags, share)
        zero_items, one_items = 2, 4
        zero_buffers, zero_sems = scratch_of(zero_items, lags, pars, members, sensors)
        one_buffers, one_sems = scratch_of(one_items, lags, pars, members, sensors)
        out = jax.ShapeDtypeStruct((1, share, sensors), jnp.float32)
        return pl.pallas_call(
            functools.partial(kernel, lags, pars, members, zero_items, one_items),
            out_shape=(out, out),
            in_specs=[pl.BlockSpec(memory_space=pl.ANY)] * 2,
            out_specs=[pl.BlockSpec(memory_space=pltpu.VMEM)] * 2,
            scratch_shapes=[
                pltpu.VMEM((sensors, panel), jnp.bfloat16),
                pltpu.VMEM((sensors, panel), jnp.bfloat16),
                pltpu.VMEM((sensors, panel), jnp.bfloat16),
                zero_buffers,
                one_buffers,
                pltpu.SemaphoreType.DMA((2,)),
                pltpu.SemaphoreType.DMA((one_items,)),
                pltpu.SemaphoreType.DMA((one_items,)),
                zero_sems,
                one_sems,
            ],
            compiler_params=pltpu.CompilerParams(
                collective_id=0, has_side_effects=True, vmem_limit_bytes=52 * 2**20
            ),
            cost_estimate=pl.CostEstimate(
                flops=4 * sensors * sensors * panel,
                bytes_accessed=4 * sensors * panel + 8 * share * sensors,
                transcendentals=0,
            ),
        )(prior_rows, raw_rows)

    in_specs = (P("lag", None, "par"), P("lag", None, "par"))
    out_specs = (P("lag", "par", None), P("lag", "par", None))
    return jax.shard_map(body, mesh=mesh, in_specs=in_specs, out_specs=out_specs, check_vma=False)
```
